32 devices in a mesh: row: 16 (over z, y, x), col: 2 (over core).
Axes of the slice: x: 2, y: 2, z: 4, core: 2. Of those that a mesh axis runs over, the one named last changes fastest.
Arguments:
- tokens: bfloat16 [2048, 1024], P('row', 'col'), may hold values from -6 to 6
- segments: int32 [2048], replicated, may hold values from 0 to 1, as said below
- first_gain: bfloat16 [1024], P('col'), may hold values from 0.5 to 1.5
- in_weight: bfloat16 [1024, 3, 1024], P('row', None, 'col'), may hold values from -0.1875 to 0.1875
- conv_kernel: bfloat16 [3, 1024], P(None, 'col'), may hold values from -4 to 4
- out_weight: bfloat16 [1024, 1024], P('row', 'col'), may hold values from -0.1875 to 0.1875
- second_gain: bfloat16 [1024], P('col'), may hold values from 0.5 to 1.5
- gate_weight: bfloat16 [1024, 4608], P('row', 'col'), may hold values from -0.1875 to 0.1875
- up_weight: bfloat16 [1024, 4608], P('row', 'col'), may hold values from -0.1875 to 0.1875
- down_weight: bfloat16 [4608, 1024], P('row', 'col'), may hold values from -0.09375 to 0.09375
- cotangent: bfloat16 [2048, 1024], P('row', 'col'), may hold values from -6 to 6
Outputs:
- block_out: bfloat16 [2048, 1024], P('row', 'col')
- tokens_grad: float32 [2048, 1024], P('row', 'col')
- first_gain_grad: float32 [1024], P('col')
- in_weight_grad: float32 [1024, 3, 1024], P('row', None, 'col')
- conv_kernel_grad: float32 [3, 1024], P(None, 'col')
- out_weight_grad: float32 [1024, 1024], P('row', 'col')
- second_gain_grad: float32 [1024], P('col')
- gate_weight_grad: float32 [1024, 4608], P('row', 'col')
- up_weight_grad: float32 [1024, 4608], P('row', 'col')
- down_weight_grad: float32 [4608, 1024], P('row', 'col')
The draws below stay inside these ranges and needn't reach their ends.
Inputs may be any that keep to these rules, and one draw needn't show every extreme that they name: `segments`: segment numbers start at 0, never fall and rise by one at each document start; the largest is reached.
All inputs are finite; a program needn't handle non-finite values.
Results may differ from the reference program's by a relative error of at most 0.0099.
Values may be sent and summed in bfloat16 or wider, within the bound.
A program may use at most 128 MiB of HBM per device.

```python
import jax
import jax.numpy as jnp
from jax import lax

D = 1024
FF = 4608
CONV = 3
TOK_DEV = 128
SPAN = 1024
TOKENS = 2048


def draw_segments(key, part):
    key = jax.random.fold_in(key, 7)
    number = TOKENS // SPAN
    jitter = jax.random.randint(key, (number,), 0, SPAN // 2)
    order = jnp.arange(number, dtype=jnp.int32)
    starts = order * SPAN + jitter
    starts = jnp.where(starts % TOK_DEV < 3, starts + 3, starts)
    starts = jnp.where(order == 0, 0, starts)
    places = jnp.arange(TOKENS, dtype=jnp.int32)
    counted = jnp.sum((places[:, None] >= starts[None, :]).astype(jnp.int32), axis=1) - 1
    return counted.astype(jnp.int32)


def level_of(own_key, dims, pieces, least, top_value):
    factor_of, own = 1.0, jax.random.fold_in(own_key, 6)
    for dim, blocks in pieces:
        steps = jnp.exp(jax.random.uniform(jax.random.fold_in(own, dim), (blocks,), jnp.float32, least / len(pieces), top_value / len(pieces)))
        factor_of = factor_of * jnp.repeat(steps, dims[dim] // blocks).reshape([-1 if axis == dim else 1 for axis in range(len(dims))])
    return factor_of


def gaussian(stream_key, shape, scale, limit, shards=(), kind=jnp.bfloat16):
    values = scale * jax.random.normal(stream_key, shape, jnp.float32)
    if shards:
        values = values * level_of(stream_key, shape, shards, -0.22, 0.18)
    return jnp.clip(values, -limit, limit).astype(kind)


def setup_inputs(seed: int = 0) -> dict:
    arg_keys = jax.random.split(jax.random.key(seed), 12)
    tokens = gaussian(arg_keys[0], (TOKENS, D), 1.0, 6.0, ((0, 16), (1, 2)))
    segments = draw_segments(jax.random.fold_in(arg_keys[11], 71), 0)
    first_gain = jnp.clip(1.0 + 0.1 * jax.random.normal(arg_keys[2], (D,), jnp.float32), 0.5, 1.5).astype(jnp.bfloat16)
    in_weight = gaussian(arg_keys[3], (D, 3, D), D ** -0.5, 0.1875, ((0, 16), (2, 2)))
    conv_kernel = gaussian(arg_keys[4], (CONV, D), 0.7, 4.0, ((1, 2),))
    out_weight = gaussian(arg_keys[5], (D, D), D ** -0.5, 0.1875, ((0, 16), (1, 2)))
    second_gain = jnp.clip(1.0 + 0.1 * jax.random.normal(arg_keys[6], (D,), jnp.float32), 0.5, 1.5).astype(jnp.bfloat16)
    gate_weight = gaussian(arg_keys[7], (D, FF), D ** -0.5, 0.1875, ((0, 16), (1, 2)))
    up_weight = gaussian(arg_keys[8], (D, FF), D ** -0.5, 0.1875, ((0, 16), (1, 2)))
    down_weight = gaussian(arg_keys[9], (FF, D), FF ** -0.5, 0.09375, ((0, 16), (1, 2)))
    cotangent = gaussian(arg_keys[10], (TOKENS, D), 1.0, 6.0, ((0, 16), (1, 2)))
    return dict(tokens=tokens, segments=segments, first_gain=first_gain, in_weight=in_weight, conv_kernel=conv_kernel, out_weight=out_weight, second_gain=second_gain, gate_weight=gate_weight, up_weight=up_weight, down_weight=down_weight, cotangent=cotangent)


epsilon = 1e-05
highest = lax.Precision.HIGHEST

@jax.custom_vjp
def low(v):
    return lax.optimization_barrier(v.astype(jnp.bfloat16)).astype(jnp.float32)

@jax.custom_vjp
def low_back(v):
    return v

def low_keep(v):
    return (low(v), None)

def low_pass(kept, grad):
    return (grad,)

def back_keep(v):
    return (v, None)

def back_low(kept, grad):
    return (low(grad),)
low.defvjp(low_keep, low_pass)
low_back.defvjp(back_keep, back_low)

def masks_of(segments):
    same_one = jnp.concatenate([jnp.zeros((1,), jnp.float32), (segments[1:] == segments[:-1]).astype(jnp.float32)])
    same_two = jnp.concatenate([jnp.zeros((2,), jnp.float32), (segments[2:] == segments[:-2]).astype(jnp.float32)])
    return (same_one[:, None], same_two[:, None])

def layer(tokens, first_gain, in_weight, conv_kernel, out_weight, second_gain, gate_weight, up_weight, down_weight, same_one, same_two):
    width = tokens.shape[1]
    inv_one = lax.rsqrt(lax.optimization_barrier(jnp.mean(tokens * tokens, axis=1, keepdims=True)) + epsilon)
    normed_one = low(tokens * inv_one * first_gain)
    projected = low_back(jnp.einsum('td,dkc->tkc', normed_one, in_weight, precision=highest))
    b_part = projected[:, 0]
    c_part = projected[:, 1]
    x_part = projected[:, 2]
    gated = b_part * x_part
    back_one = jnp.concatenate([jnp.zeros((1, width), jnp.float32), gated[:-1]]) * same_one
    back_two = jnp.concatenate([jnp.zeros((2, width), jnp.float32), gated[:-2]]) * same_two
    mixed = conv_kernel[0] * gated + conv_kernel[1] * back_one + conv_kernel[2] * back_two
    conv_out = low(c_part * mixed)
    attended = low_back(jnp.dot(conv_out, out_weight, precision=highest))
    middle = tokens + attended
    inv_two = lax.rsqrt(lax.optimization_barrier(jnp.mean(middle * middle, axis=1, keepdims=True)) + epsilon)
    normed_two = low(middle * inv_two * second_gain)
    gate_value = low_back(jnp.dot(normed_two, gate_weight, precision=highest))
    up_value = low_back(jnp.dot(normed_two, up_weight, precision=highest))
    hidden = low(jax.nn.silu(gate_value) * up_value)
    return middle + jnp.dot(hidden, down_weight, precision=highest)

def reference(tokens, segments, first_gain, in_weight, conv_kernel, out_weight, second_gain, gate_weight, up_weight, down_weight, cotangent):
    same_one, same_two = masks_of(segments)
    floats = [array.astype(jnp.float32) for array in (tokens, first_gain, in_weight, conv_kernel, out_weight, second_gain, gate_weight, up_weight, down_weight)]

    def forward(*values):
        return layer(*values, same_one, same_two)
    result, pullback = jax.vjp(forward, *floats)
    grads = pullback(cotangent.astype(jnp.float32))
    return (result.astype(jnp.bfloat16), grads[0], grads[1], grads[2], grads[3], grads[4], grads[5], grads[6], grads[7], grads[8])
```

```python
import functools

import jax
import jax.numpy as jnp
from jax import lax
from jax.experimental import pallas as pl
from jax.experimental.pallas import tpu as pltpu
from jax.sharding import PartitionSpec as P

D = 1024


epsilon = 1e-05


def shifted(block, axis, distance):
    devices = range(lax.axis_size(axis))
    route = [(i - distance, i) for i in devices if i - distance in devices]
    return lax.ppermute(block, axis, route)


def widen(values):
    return lax.all_gather(values, "col", axis=1, tiled=True)


def squares_inverse(values):
    total = lax.psum(jnp.sum(values * values, axis=1), "col")
    return lax.rsqrt(total / D + epsilon)[:, None]


def norm_backward(grad, gain, values, inverse):
    scaled = grad * gain
    total = lax.psum(jnp.sum(scaled * values, axis=1), "col")
    back = inverse * scaled - values * inverse**3 * (total[:, None] / D)
    return (back, jnp.sum(grad * values * inverse, axis=0))


def project(left, weight):
    return jnp.einsum("td,dkc->tkc", left, weight, preferred_element_type=jnp.float32)


def pull(grad, weight):
    partial_sum = jnp.einsum("tkc,dkc->td", grad, weight, preferred_element_type=jnp.float32)
    return lax.psum_scatter(partial_sum, "col", scatter_dimension=1, tiled=True)


def weight_terms(left, grad):
    return lax.psum_scatter(
        jnp.einsum("tr,tkc->rkc", left, grad, preferred_element_type=jnp.float32),
        "row",
        scatter_dimension=0,
        tiled=True,
    )


def local(
    tokens,
    segments,
    first_gain,
    in_weight,
    conv_kernel,
    out_weight,
    second_gain,
    gate_weight,
    up_weight,
    down_weight,
    cotangent,
):
    rows_here = tokens.shape[0]
    tok_float = tokens.astype(jnp.float32)
    gain_one = first_gain.astype(jnp.float32)
    gain_two = second_gain.astype(jnp.float32)
    kernel = conv_kernel.astype(jnp.float32)
    in_full, out_full, gate_full, up_full, down_full = (
        lax.all_gather(in_weight, "row", axis=0, tiled=True),
        lax.all_gather(out_weight, "row", axis=0, tiled=True),
        lax.all_gather(gate_weight, "row", axis=0, tiled=True),
        lax.all_gather(up_weight, "row", axis=0, tiled=True),
        lax.all_gather(down_weight, "row", axis=0, tiled=True),
    )
    pair_weights = jnp.stack([gate_full, up_full], axis=1)
    inv_one = squares_inverse(tok_float)
    normed_one = (tok_float * inv_one * gain_one).astype(jnp.bfloat16)
    normed_one_full = widen(normed_one)
    projected = project(normed_one_full, in_full)
    b_part = projected[:, 0]
    c_part = projected[:, 1]
    x_part = projected[:, 2]
    gated = b_part * x_part
    first_row = lax.axis_index("row") * rows_here
    padded = jnp.concatenate(
        [jnp.full((2,), -1, jnp.int32), segments, jnp.full((2,), -2, jnp.int32)]
    )
    window = lax.dynamic_slice_in_dim(padded, first_row, rows_here + 4)
    own_ids = window[2 : rows_here + 2]
    same_one = (own_ids == window[1 : rows_here + 1]).astype(jnp.float32)[:, None]
    same_two = (own_ids == window[0:rows_here]).astype(jnp.float32)[:, None]
    after_one = (window[3 : rows_here + 3] == own_ids).astype(jnp.float32)[:, None]
    after_two = (window[4 : rows_here + 4] == own_ids).astype(jnp.float32)[:, None]
    earlier = shifted(gated[rows_here - 2 :], "row", 1)
    extended = jnp.concatenate([earlier, gated], axis=0)
    back_one = extended[1 : rows_here + 1] * same_one
    back_two = extended[0:rows_here] * same_two
    mixed = kernel[0] * gated + kernel[1] * back_one + kernel[2] * back_two
    conv_out = (c_part * mixed).astype(jnp.bfloat16)
    conv_full = widen(conv_out)
    attended = project(conv_full, out_full[:, None, :])[:, 0]
    middle = tok_float + attended
    inv_two = squares_inverse(middle)
    normed_two = (middle * inv_two * gain_two).astype(jnp.bfloat16)
    normed_two_full = widen(normed_two)
    both_values = project(normed_two_full, pair_weights)
    gate_value = both_values[:, 0]
    up_value = both_values[:, 1]
    sigma = jax.nn.sigmoid(gate_value)
    activated = gate_value * sigma
    hidden = (activated * up_value).astype(jnp.bfloat16)
    hidden_full = widen(hidden)
    branch_out = project(hidden_full, down_full[:, None, :])[:, 0]
    block_out = (middle + branch_out).astype(jnp.bfloat16)
    cot_three = cotangent[:, None, :]
    hidden_grad = pull(cot_three, down_full[:, None, :])
    down_grad = weight_terms(hidden_full, cot_three)[:, 0]
    gate_grad = hidden_grad * up_value * sigma * (1.0 + gate_value * (1.0 - sigma))
    up_grad = hidden_grad * activated
    pair_grad = jnp.stack([gate_grad, up_grad], axis=1).astype(jnp.bfloat16)
    normed_two_grad = pull(pair_grad, pair_weights)
    pair_weight_grad = weight_terms(normed_two_full, pair_grad)
    middle_back, gain_two_local = norm_backward(normed_two_grad, gain_two, middle, inv_two)
    middle_grad = cotangent.astype(jnp.float32) + middle_back
    attended_grad = middle_grad.astype(jnp.bfloat16)[:, None, :]
    conv_grad = pull(attended_grad, out_full[:, None, :])
    out_grad = weight_terms(conv_full, attended_grad)[:, 0]
    c_grad = conv_grad * mixed
    mixed_grad = conv_grad * c_part
    later = shifted(mixed_grad[0:2], "row", -1)
    ahead = jnp.concatenate([mixed_grad, later], axis=0)
    gated_grad = (
        kernel[0] * mixed_grad
        + kernel[1] * after_one * ahead[1 : rows_here + 1]
        + kernel[2] * after_two * ahead[2 : rows_here + 2]
    )
    kernel_local = jnp.stack(
        [
            jnp.sum(mixed_grad * gated, axis=0),
            jnp.sum(mixed_grad * back_one, axis=0),
            jnp.sum(mixed_grad * back_two, axis=0),
        ]
    )
    projected_grad = jnp.stack([gated_grad * x_part, c_grad, gated_grad * b_part], axis=1).astype(
        jnp.bfloat16
    )
    normed_one_grad = pull(projected_grad, in_full)
    in_grad = weight_terms(normed_one_full, projected_grad)
    token_back, gain_one_local = norm_backward(normed_one_grad, gain_one, tok_float, inv_one)
    tokens_grad = middle_grad + token_back
    gain_one_grad, kernel_grad, gain_two_grad = lax.psum(
        (gain_one_local, kernel_local, gain_two_local), "row"
    )
    return (
        block_out,
        tokens_grad,
        gain_one_grad,
        in_grad,
        kernel_grad,
        out_grad,
        gain_two_grad,
        pair_weight_grad[:, 0],
        pair_weight_grad[:, 1],
        down_grad,
    )


MESH = pl.DeviceIdType.MESH
VMEM = pl.BlockSpec(memory_space=pltpu.VMEM)
ANY = pl.BlockSpec(memory_space=pl.ANY)


def greet(devices):
    barrier = pltpu.get_barrier_semaphore()
    for device in devices:
        pl.semaphore_signal(barrier, inc=1, device_id=device, device_id_type=MESH)
    pl.semaphore_wait(barrier, len(devices))


def remote(source, target, send, receive, device):
    return pltpu.make_async_remote_copy(
        src_ref=source,
        dst_ref=target,
        send_sem=send,
        recv_sem=receive,
        device_id=device,
        device_id_type=MESH,
    )


def gather_kernel(team, cols, count, *refs):
    ins, outs = refs[:count], refs[count : 2 * count]
    send, recv, pass_send, pass_recv, own_sem = refs[2 * count :]
    row, col = lax.axis_index("row"), lax.axis_index("col")
    place = lax.rem(row, team)
    first = row - place
    mates = [first + lax.rem(place + k, team) for k in range(1, team)]
    others = [lax.rem(col + j, cols) for j in range(1, cols)]
    greet([(mate, col) for mate in mates] + [(row, other) for other in others])

    def slot(i, which, side):
        tall, wide = ins[i].shape
        return outs[i].at[
            pl.ds(pl.multiple_of(which * tall, tall), tall),
            pl.ds(pl.multiple_of(side * wide, wide), wide),
        ]

    sends, passes, locals_ = {}, {}, []
    for i in range(count):
        for k in range(1, team):
            sends[i, k] = remote(
                ins[i], slot(i, place, col), send.at[i, k], recv.at[i, k], (mates[k - 1], col)
            )
            sends[i, k].start()
        for j in range(1, cols):
            passes[i, 0, j] = remote(
                ins[i],
                slot(i, place, col),
                pass_send.at[i, 0, j],
                pass_recv.at[i, 0, j],
                (row, others[j - 1]),
            )
            passes[i, 0, j].start()
        copy = pltpu.make_async_copy(ins[i], slot(i, place, col), own_sem.at[i])
        copy.start()
        locals_.append(copy)
    for i in range(count):
        for k in range(1, team):
            origin = lax.rem(place - k + team, team)
            arrived = slot(i, origin, col)
            remote(arrived, arrived, send.at[i, k], recv.at[i, k], (mates[k - 1], col)).wait_recv()
            for j in range(1, cols):
                passes[i, k, j] = remote(
                    arrived,
                    arrived,
                    pass_send.at[i, k, j],
                    pass_recv.at[i, k, j],
                    (row, others[j - 1]),
                )
                passes[i, k, j].start()
    for (i, k, j), copy in passes.items():
        origin = lax.rem(place - k + team, team)
        landed = slot(i, origin, lax.rem(col - j + cols, cols))
        remote(
            landed, landed, pass_send.at[i, k, j], pass_recv.at[i, k, j], (row, others[j - 1])
        ).wait_recv()
    for copy in passes.values():
        copy.wait_send()
    for copy in sends.values():
        copy.wait_send()
    for copy in locals_:
        copy.wait()


def gather(blocks, team, cols, identity):
    count = len(blocks)
    return pl.pallas_call(
        functools.partial(gather_kernel, team, cols, count),
        out_shape=[
            jax.ShapeDtypeStruct((b.shape[0] * team, b.shape[1] * cols), b.dtype) for b in blocks
        ],
        in_specs=[ANY] * count,
        out_specs=[ANY] * count,
        scratch_shapes=[
            pltpu.SemaphoreType.DMA((count, team)),
            pltpu.SemaphoreType.DMA((count, team)),
            pltpu.SemaphoreType.DMA((count, team, cols)),
            pltpu.SemaphoreType.DMA((count, team, cols)),
            pltpu.SemaphoreType.DMA((count,)),
        ],
        compiler_params=pltpu.CompilerParams(collective_id=identity, has_side_effects=True),
    )(*blocks)


def scatter_kernel(
    team, cols, x_ref, o_ref, inbox, stage, land, send, recv, pass_send, pass_recv
):
    row, col = lax.axis_index("row"), lax.axis_index("col")
    place = lax.rem(row, team)
    first = row - place
    mates = [first + lax.rem(place + k, team) for k in range(1, team)]
    others = [lax.rem(col + j, cols) for j in range(1, cols)]
    greet([(mate, col) for mate in mates] + [(row, other) for other in others])
    tall, wide = o_ref.shape

    def part(k, side):
        return x_ref.at[
            pl.ds(pl.multiple_of(lax.rem(place + k, team) * tall, tall), tall),
            pl.ds(pl.multiple_of(side * wide, wide), wide),
        ]

    order = list(range(1, team)) + [0]
    passes, sends = {}, {}
    for k in order:
        for j in range(1, cols):
            passes[k, j] = remote(
                part(k, others[j - 1]),
                inbox.at[j - 1, k],
                pass_send.at[k, j],
                pass_recv.at[k, j],
                (row, others[j - 1]),
            )
            passes[k, j].start()
    for k in order:
        total = part(k, col)[...].astype(jnp.float32)
        for j in range(1, cols):
            passes[k, j].wait_recv()
            total = total + inbox[j - 1, k].astype(jnp.float32)
        if k:
            stage[k - 1] = total.astype(jnp.bfloat16)
            sends[k] = remote(
                stage.at[k - 1], land.at[k - 1], send.at[k], recv.at[k], (mates[k - 1], col)
            )
            sends[k].start()
        else:
            o_ref[...] = total
    for k in range(1, team):
        sends[k].wait_recv()
        o_ref[...] += land[k - 1].astype(jnp.float32)
    for copy in passes.values():
        copy.wait_send()
    for copy in sends.values():
        copy.wait_send()


def scatter(partial_sum, team, cols, identity):
    tall, wide = partial_sum.shape[0] // team, partial_sum.shape[1] // cols
    return pl.pallas_call(
        functools.partial(scatter_kernel, team, cols),
        out_shape=jax.ShapeDtypeStruct((tall, wide), jnp.float32),
        in_specs=[VMEM],
        out_specs=VMEM,
        scratch_shapes=[
            pltpu.VMEM((cols - 1, team, tall, wide), jnp.bfloat16),
            pltpu.VMEM((team - 1, tall, wide), jnp.bfloat16),
            pltpu.VMEM((team - 1, tall, wide), jnp.bfloat16),
            pltpu.SemaphoreType.DMA((team,)),
            pltpu.SemaphoreType.DMA((team,)),
            pltpu.SemaphoreType.DMA((team, cols)),
            pltpu.SemaphoreType.DMA((team, cols)),
        ],
        compiler_params=pltpu.CompilerParams(
            collective_id=identity, has_side_effects=True, vmem_limit_bytes=24 * 2**20
        ),
    )(partial_sum)


def exchange_kernel(
    team, cols, outward, wide_ref, tall_ref, wide_out, tall_out, send, recv, t_send, t_recv, own
):
    rows = team * cols
    row, col = lax.axis_index("row"), lax.axis_index("col")
    place = lax.rem(row, team)
    group = lax.div(row, team)
    peers = [lax.rem(row + k, rows) for k in range(1, rows)]
    greet(
        [(peer, col) for peer in peers]
        + [
            (lax.rem(group + m, cols) * team + place, lax.rem(col + j, cols))
            for m in range(cols)
            for j in range(1, cols)
        ]
    )
    home = group == col

    def target(m):
        if outward:
            return lax.rem(group + m, cols) * team + place, group
        return col * team + place, lax.rem(col + m, cols)

    def tall_copy(m):
        if outward:
            source, landing, index = tall_ref, tall_out.at[col], col
        else:
            source, landing, index = tall_ref.at[lax.rem(col + m, cols)], tall_out.at[group], group
        return remote(source, landing, t_send.at[m], t_recv.at[index], target(m))

    def tall_own():
        source = tall_ref if outward else tall_ref.at[col]
        return pltpu.make_async_copy(source, tall_out.at[col], own.at[1])

    def wide_source(peer):
        return wide_ref.at[lax.rem(peer, team) if outward else peer]

    copies = []
    for k in range(1, rows):
        peer = peers[k - 1]
        copy = remote(
            wide_source(peer), wide_out.at[row], send.at[k], recv.at[k], (peer, col)
        )
        copy.start()
        copies.append(copy)
    mine = pltpu.make_async_copy(wide_source(row), wide_out.at[row], own.at[0])
    mine.start()
    for m in range(cols):
        if m:
            tall_copy(m).start()
        else:
            pl.when(home)(lambda: tall_own().start())
            pl.when(jnp.logical_not(home))(lambda: tall_copy(0).start())
    for k in range(1, rows):
        landed = wide_out.at[lax.rem(row - k + rows, rows)]
        remote(landed, landed, send.at[k], recv.at[k], (peers[k - 1], col)).wait_recv()
    for j in range(cols):
        landed = tall_out.at[j]
        arriving = remote(landed, landed, t_send.at[0], t_recv.at[j], target(1))
        is_own = jnp.logical_and(home, col == j)
        pl.when(is_own)(lambda: tall_own().wait())
        pl.when(jnp.logical_not(is_own))(lambda arriving=arriving: arriving.wait_recv())
    for copy in copies:
        copy.wait_send()
    mine.wait()
    for m in range(cols):
        if m:
            tall_copy(m).wait_send()
        else:
            pl.when(jnp.logical_not(home))(lambda: tall_copy(0).wait_send())


def exchange(wide, tall, team, cols, outward, identity):
    rows = team * cols
    return pl.pallas_call(
        functools.partial(exchange_kernel, team, cols, outward),
        out_shape=[
            jax.ShapeDtypeStruct((rows,) + wide.shape[1:], wide.dtype),
            jax.ShapeDtypeStruct((cols,) + tall.shape[-2:], tall.dtype),
        ],
        in_specs=[ANY] * 2,
        out_specs=[ANY] * 2,
        scratch_shapes=[
            pltpu.SemaphoreType.DMA((rows,)),
            pltpu.SemaphoreType.DMA((rows,)),
            pltpu.SemaphoreType.DMA((cols,)),
            pltpu.SemaphoreType.DMA((cols,)),
            pltpu.SemaphoreType.DMA((2,)),
        ],
        compiler_params=pltpu.CompilerParams(collective_id=identity, has_side_effects=True),
    )(wide, tall)


def dot(a, b, a_dim, b_dim, kind=jnp.float32):
    out = lax.dot_general(
        a, b, (((a_dim,), (b_dim,)), ((), ())), preferred_element_type=jnp.float32
    )
    return out.astype(kind)


def teams(
    tokens,
    segments,
    first_gain,
    in_weight,
    conv_kernel,
    out_weight,
    second_gain,
    gate_weight,
    up_weight,
    down_weight,
    cotangent,
):
    bf = jnp.bfloat16
    rows, cols = lax.axis_size("row"), lax.axis_size("col")
    team = rows // cols
    row, col = lax.axis_index("row"), lax.axis_index("col")
    place, group = lax.rem(row, team), lax.div(row, team)
    depth, _, width = in_weight.shape
    inner = gate_weight.shape[1]
    thin, part = width // team, inner // team
    held = tokens.shape[0] * team
    blocks = in_weight.reshape(depth, 3, team, thin).transpose(2, 0, 1, 3)
    wide = jnp.concatenate(
        [
            blocks.reshape(team, depth, 3 * thin),
            gate_weight.reshape(depth, team, part).transpose(1, 0, 2),
            up_weight.reshape(depth, team, part).transpose(1, 0, 2),
        ],
        axis=2,
    )
    tall = jnp.concatenate([out_weight, down_weight], axis=0)
    tok_float = tokens.astype(jnp.float32)
    gain_one = first_gain.astype(jnp.float32)
    gain_two = second_gain.astype(jnp.float32)
    kernel = lax.dynamic_slice_in_dim(conv_kernel, place * thin, thin, 1).astype(jnp.float32)
    inv_one = squares_inverse(tok_float)
    normed_one = (tok_float * inv_one * gain_one).astype(bf)

    wide_all, tall_all = exchange(wide, tall, team, cols, True, 1)
    wide_all = wide_all.reshape(rows * depth, 3 * thin + 2 * part)
    in_part, pair_part = wide_all[:, : 3 * thin], wide_all[:, 3 * thin :]
    tall_all = tall_all.transpose(1, 0, 2).reshape(tall.shape[0], cols * width)
    out_part, down_part = tall_all[:depth], tall_all[depth:]
    normed_full, cot_full = gather([normed_one, cotangent], team, cols, 2)

    projected = dot(normed_full, in_part, 1, 0)
    b_part = projected[:, :thin]
    c_part = projected[:, thin : 2 * thin]
    x_part = projected[:, 2 * thin :]
    gated = b_part * x_part
    padded = jnp.concatenate(
        [jnp.full((2,), -1, jnp.int32), segments, jnp.full((2,), -2, jnp.int32)]
    )
    window = lax.dynamic_slice_in_dim(padded, group * held, held + 4)
    own_ids = window[2 : held + 2]
    same_one = (own_ids == window[1 : held + 1]).astype(jnp.float32)[:, None]
    same_two = (own_ids == window[0:held]).astype(jnp.float32)[:, None]
    after_one = (window[3 : held + 3] == own_ids).astype(jnp.float32)[:, None]
    after_two = (window[4 : held + 4] == own_ids).astype(jnp.float32)[:, None]
    earlier = shifted(gated[held - 2 :], "row", team)
    extended = jnp.concatenate([earlier, gated], axis=0)
    back_one = extended[1 : held + 1] * same_one
    back_two = extended[0:held] * same_two
    mixed = kernel[0] * gated + kernel[1] * back_one + kernel[2] * back_two
    conv_out = (c_part * mixed).astype(bf)
    attended = scatter(dot(conv_out, out_part, 1, 0, bf), team, cols, 3)
    middle = tok_float + attended
    inv_two = squares_inverse(middle)
    normed_two = (middle * inv_two * gain_two).astype(bf)
    (two_full,) = gather([normed_two], team, cols, 4)
    both = dot(two_full, pair_part, 1, 0)
    gate_value, up_value = both[:, :part], both[:, part:]
    sigma = jax.nn.sigmoid(gate_value)
    activated = gate_value * sigma
    hidden = (activated * up_value).astype(bf)
    hidden_grad = dot(cot_full, down_part, 1, 1)
    gate_grad = hidden_grad * up_value * sigma * (1.0 + gate_value * (1.0 - sigma))
    up_grad = hidden_grad * activated
    pair_grad = jnp.concatenate([gate_grad.astype(bf), up_grad.astype(bf)], axis=1)
    normed_two_grad = scatter(dot(pair_grad, pair_part, 1, 1, bf), team, cols, 5)
    branch_out = scatter(dot(hidden, down_part, 1, 0, bf), team, cols, 6)
    block_out = (middle + branch_out).astype(bf)
    middle_back, gain_two_local = norm_backward(normed_two_grad, gain_two, middle, inv_two)
    middle_grad = cotangent.astype(jnp.float32) + middle_back
    (attended_grad,) = gather([middle_grad.astype(bf)], team, cols, 7)
    conv_grad = dot(attended_grad, out_part, 1, 1)
    c_grad = conv_grad * mixed
    mixed_grad = conv_grad * c_part
    later = shifted(mixed_grad[0:2], "row", -team)
    ahead = jnp.concatenate([mixed_grad, later], axis=0)
    gated_grad = (
        kernel[0] * mixed_grad
        + kernel[1] * after_one * ahead[1 : held + 1]
        + kernel[2] * after_two * ahead[2 : held + 2]
    )
    kernel_local = jnp.stack(
        [
            jnp.sum(mixed_grad * gated, axis=0),
            jnp.sum(mixed_grad * back_one, axis=0),
            jnp.sum(mixed_grad * back_two, axis=0),
        ]
    )
    kernel_local = lax.dynamic_update_slice_in_dim(
        jnp.zeros((3, width), jnp.float32), kernel_local, place * thin, 1
    )
    projected_grad = jnp.concatenate(
        [
            (gated_grad * x_part).astype(bf),
            c_grad.astype(bf),
            (gated_grad * b_part).astype(bf),
        ],
        axis=1,
    )
    normed_one_grad = scatter(dot(projected_grad, in_part, 1, 1, bf), team, cols, 8)
    token_back, gain_one_local = norm_backward(normed_one_grad, gain_one, tok_float, inv_one)
    tokens_grad = middle_grad + token_back

    wide_grad = jnp.concatenate(
        [dot(normed_full, projected_grad, 0, 0, bf), dot(two_full, pair_grad, 0, 0, bf)], axis=1
    ).reshape(rows, depth, 3 * thin + 2 * part)
    tall_grad = jnp.concatenate(
        [dot(conv_out, attended_grad, 0, 0, bf), dot(hidden, cot_full, 0, 0, bf)], axis=0
    )
    tall_grad = tall_grad.reshape(tall.shape[0], cols, width).transpose(1, 0, 2)
    wide_back, tall_back = exchange(wide_grad, tall_grad, team, cols, False, 9)
    wide_sum = jnp.sum(
        wide_back.astype(jnp.float32).reshape(cols, team, depth, 3 * thin + 2 * part), axis=0
    )
    tall_sum = jnp.sum(tall_back.astype(jnp.float32), axis=0)
    in_grad = (
        wide_sum[:, :, : 3 * thin]
        .reshape(team, depth, 3, thin)
        .transpose(1, 2, 0, 3)
        .reshape(in_weight.shape)
    )
    gate_out = wide_sum[:, :, 3 * thin : 3 * thin + part].transpose(1, 0, 2).reshape(depth, inner)
    up_out = wide_sum[:, :, 3 * thin + part :].transpose(1, 0, 2).reshape(depth, inner)
    gain_one_grad, kernel_grad, gain_two_grad = lax.psum(
        (gain_one_local, kernel_local, gain_two_local), "row"
    )
    return (
        block_out,
        tokens_grad,
        gain_one_grad,
        in_grad,
        kernel_grad,
        tall_sum[:depth],
        gain_two_grad,
        gate_out,
        up_out,
        tall_sum[depth:],
    )


def solution(mesh):
    in_specs = (
        P("row", "col"),
        P(),
        P("col"),
        P("row", None, "col"),
        P(None, "col"),
        P("row", "col"),
        P("col"),
        P("row", "col"),
        P("row", "col"),
        P("row", "col"),
        P("row", "col"),
    )
    out_specs = (
        P("row", "col"),
        P("row", "col"),
        P("col"),
        P("row", None, "col"),
        P(None, "col"),
        P("row", "col"),
        P("col"),
        P("row", "col"),
        P("row", "col"),
        P("row", "col"),
    )
    rows, cols = mesh.shape["row"], mesh.shape["col"]
    shared = cols > 1 and rows % cols == 0 and rows // cols > 1
    body = teams if shared else local
    return jax.shard_map(body, mesh=mesh, in_specs=in_specs, out_specs=out_specs, check_vma=False)
```

```python
import functools

import jax
import jax.numpy as jnp
from jax import lax
from jax.experimental import pallas as pl
from jax.experimental.pallas import tpu as pltpu
from jax.sharding import PartitionSpec as P

D = 1024


epsilon = 1e-05


def shifted(block, axis, distance):
    devices = range(lax.axis_size(axis))
    route = [(i - distance, i) for i in devices if i - distance in devices]
    return lax.ppermute(block, axis, route)


def widen(values):
    return lax.all_gather(values, "col", axis=1, tiled=True)


def squares_inverse(values):
    total = lax.psum(jnp.sum(values * values, axis=1), "col")
    return lax.rsqrt(total / D + epsilon)[:, None]


def norm_backward(grad, gain, values, inverse):
    scaled = grad * gain
    total = lax.psum(jnp.sum(scaled * values, axis=1), "col")
    back = inverse * scaled - values * inverse**3 * (total[:, None] / D)
    return (back, jnp.sum(grad * values * inverse, axis=0))


def project(left, weight):
    return jnp.einsum("td,dkc->tkc", left, weight, preferred_element_type=jnp.float32)


def pull(grad, weight):
    partial_sum = jnp.einsum("tkc,dkc->td", grad, weight, preferred_element_type=jnp.float32)
    return lax.psum_scatter(partial_sum, "col", scatter_dimension=1, tiled=True)


def weight_terms(left, grad):
    return lax.psum_scatter(
        jnp.einsum("tr,tkc->rkc", left, grad, preferred_element_type=jnp.float32),
        "row",
        scatter_dimension=0,
        tiled=True,
    )


def local(
    tokens,
    segments,
    first_gain,
    in_weight,
    conv_kernel,
    out_weight,
    second_gain,
    gate_weight,
    up_weight,
    down_weight,
    cotangent,
):
    rows_here = tokens.shape[0]
    tok_float = tokens.astype(jnp.float32)
    gain_one = first_gain.astype(jnp.float32)
    gain_two = second_gain.astype(jnp.float32)
    kernel = conv_kernel.astype(jnp.float32)
    in_full, out_full, gate_full, up_full, down_full = (
        lax.all_gather(in_weight, "row", axis=0, tiled=True),
        lax.all_gather(out_weight, "row", axis=0, tiled=True),
        lax.all_gather(gate_weight, "row", axis=0, tiled=True),
        lax.all_gather(up_weight, "row", axis=0, tiled=True),
        lax.all_gather(down_weight, "row", axis=0, tiled=True),
    )
    pair_weights = jnp.stack([gate_full, up_full], axis=1)
    inv_one = squares_inverse(tok_float)
    normed_one = (tok_float * inv_one * gain_one).astype(jnp.bfloat16)
    normed_one_full = widen(normed_one)
    projected = project(normed_one_full, in_full)
    b_part = projected[:, 0]
    c_part = projected[:, 1]
    x_part = projected[:, 2]
    gated = b_part * x_part
    first_row = lax.axis_index("row") * rows_here
    padded = jnp.concatenate(
        [jnp.full((2,), -1, jnp.int32), segments, jnp.full((2,), -2, jnp.int32)]
    )
    window = lax.dynamic_slice_in_dim(padded, first_row, rows_here + 4)
    own_ids = window[2 : rows_here + 2]
    same_one = (own_ids == window[1 : rows_here + 1]).astype(jnp.float32)[:, None]
    same_two = (own_ids == window[0:rows_here]).astype(jnp.float32)[:, None]
    after_one = (window[3 : rows_here + 3] == own_ids).astype(jnp.float32)[:, None]
    after_two = (window[4 : rows_here + 4] == own_ids).astype(jnp.float32)[:, None]
    earlier = shifted(gated[rows_here - 2 :], "row", 1)
    extended = jnp.concatenate([earlier, gated], axis=0)
    back_one = extended[1 : rows_here + 1] * same_one
    back_two = extended[0:rows_here] * same_two
    mixed = kernel[0] * gated + kernel[1] * back_one + kernel[2] * back_two
    conv_out = (c_part * mixed).astype(jnp.bfloat16)
    conv_full = widen(conv_out)
    attended = project(conv_full, out_full[:, None, :])[:, 0]
    middle = tok_float + attended
    inv_two = squares_inverse(middle)
    normed_two = (middle * inv_two * gain_two).astype(jnp.bfloat16)
    normed_two_full = widen(normed_two)
    both_values = project(normed_two_full, pair_weights)
    gate_value = both_values[:, 0]
    up_value = both_values[:, 1]
    sigma = jax.nn.sigmoid(gate_value)
    activated = gate_value * sigma
    hidden = (activated * up_value).astype(jnp.bfloat16)
    hidden_full = widen(hidden)
    branch_out = project(hidden_full, down_full[:, None, :])[:, 0]
    block_out = (middle + branch_out).astype(jnp.bfloat16)
    cot_three = cotangent[:, None, :]
    hidden_grad = pull(cot_three, down_full[:, None, :])
    down_grad = weight_terms(hidden_full, cot_three)[:, 0]
    gate_grad = hidden_grad * up_value * sigma * (1.0 + gate_value * (1.0 - sigma))
    up_grad = hidden_grad * activated
    pair_grad = jnp.stack([gate_grad, up_grad], axis=1).astype(jnp.bfloat16)
    normed_two_grad = pull(pair_grad, pair_weights)
    pair_weight_grad = weight_terms(normed_two_full, pair_grad)
    middle_back, gain_two_local = norm_backward(normed_two_grad, gain_two, middle, inv_two)
    middle_grad = cotangent.astype(jnp.float32) + middle_back
    attended_grad = middle_grad.astype(jnp.bfloat16)[:, None, :]
    conv_grad = pull(attended_grad, out_full[:, None, :])
    out_grad = weight_terms(conv_full, attended_grad)[:, 0]
    c_grad = conv_grad * mixed
    mixed_grad = conv_grad * c_part
    later = shifted(mixed_grad[0:2], "row", -1)
    ahead = jnp.concatenate([mixed_grad, later], axis=0)
    gated_grad = (
        kernel[0] * mixed_grad
        + kernel[1] * after_one * ahead[1 : rows_here + 1]
        + kernel[2] * after_two * ahead[2 : rows_here + 2]
    )
    kernel_local = jnp.stack(
        [
            jnp.sum(mixed_grad * gated, axis=0),
            jnp.sum(mixed_grad * back_one, axis=0),
            jnp.sum(mixed_grad * back_two, axis=0),
        ]
    )
    projected_grad = jnp.stack([gated_grad * x_part, c_grad, gated_grad * b_part], axis=1).astype(
        jnp.bfloat16
    )
    normed_one_grad = pull(projected_grad, in_full)
    in_grad = weight_terms(normed_one_full, projected_grad)
    token_back, gain_one_local = norm_backward(normed_one_grad, gain_one, tok_float, inv_one)
    tokens_grad = middle_grad + token_back
    gain_one_grad, kernel_grad, gain_two_grad = lax.psum(
        (gain_one_local, kernel_local, gain_two_local), "row"
    )
    return (
        block_out,
        tokens_grad,
        gain_one_grad,
        in_grad,
        kernel_grad,
        out_grad,
        gain_two_grad,
        pair_weight_grad[:, 0],
        pair_weight_grad[:, 1],
        down_grad,
    )


MESH = pl.DeviceIdType.MESH
VMEM = pl.BlockSpec(memory_space=pltpu.VMEM)
ANY = pl.BlockSpec(memory_space=pl.ANY)


def greet(devices):
    barrier = pltpu.get_barrier_semaphore()
    for device in devices:
        pl.semaphore_signal(barrier, inc=1, device_id=device, device_id_type=MESH)
    pl.semaphore_wait(barrier, len(devices))


def remote(source, target, send, receive, device):
    return pltpu.make_async_remote_copy(
        src_ref=source,
        dst_ref=target,
        send_sem=send,
        recv_sem=receive,
        device_id=device,
        device_id_type=MESH,
    )


class Here:
    def __init__(self, team, cols):
        self.team, self.cols, self.rows = team, cols, team * cols
        self.row, self.col = lax.axis_index("row"), lax.axis_index("col")
        self.place, self.group = lax.rem(self.row, team), lax.div(self.row, team)
        first = self.row - self.place
        self.mates = [None] + [first + lax.rem(self.place + k, team) for k in range(1, team)]
        self.others = [None] + [lax.rem(self.col + j, cols) for j in range(1, cols)]
        self.peers = [None] + [lax.rem(self.row + k, self.rows) for k in range(1, self.rows)]

    def greet(self):
        devices = [(peer, self.col) for peer in self.peers[1:]]
        for m in range(self.cols):
            there = lax.rem(self.group + m, self.cols) * self.team + self.place
            devices += [(there, other) for other in self.others[1:]]
        barrier = pltpu.get_barrier_semaphore()
        for device in devices:
            pl.semaphore_signal(barrier, inc=1, device_id=device, device_id_type=MESH)
        pl.semaphore_wait(barrier, len(devices))


class Gather:
    def __init__(self, block, team, cols):
        self.operands, self.in_specs, self.out_specs = [block], [ANY], [ANY]
        tall, wide = block.shape
        self.out_shape = [jax.ShapeDtypeStruct((tall * team, wide * cols), block.dtype)]
        self.scratch = [
            pltpu.SemaphoreType.DMA((team,)),
            pltpu.SemaphoreType.DMA((team,)),
            pltpu.SemaphoreType.DMA((team, cols)),
            pltpu.SemaphoreType.DMA((team, cols)),
            pltpu.SemaphoreType.DMA((1,)),
        ]

    def bind(self, here, x_ref, o_ref, send, recv, pass_send, pass_recv, own):
        self.here, self.x_ref, self.o_ref = here, x_ref, o_ref
        self.send, self.recv = send, recv
        self.pass_send, self.pass_recv, self.own = pass_send, pass_recv, own

    def slot(self, k, side):
        tall, wide = self.x_ref.shape
        origin = lax.rem(self.here.place - k + self.here.team, self.here.team)
        return self.o_ref.at[
            pl.ds(pl.multiple_of(origin * tall, tall), tall),
            pl.ds(pl.multiple_of(side * wide, wide), wide),
        ]

    def row_copy(self, source, target, k):
        device = (self.here.mates[k], self.here.col)
        return remote(source, target, self.send.at[k], self.recv.at[k], device)

    def col_copy(self, source, target, k, j):
        device = (self.here.row, self.here.others[j])
        return remote(source, target, self.pass_send.at[k, j], self.pass_recv.at[k, j], device)

    def start(self):
        here = self.here
        mine = self.slot(0, here.col)
        self.sends = [self.row_copy(self.x_ref, mine, k) for k in range(1, here.team)]
        self.passes = [self.col_copy(self.x_ref, mine, 0, j) for j in range(1, here.cols)]
        self.mine = pltpu.make_async_copy(self.x_ref, mine, self.own.at[0])
        for copy in self.sends + self.passes + [self.mine]:
            copy.start()

    def middle(self):
        here = self.here
        for k in range(1, here.team):
            arrived = self.slot(k, here.col)
            self.row_copy(arrived, arrived, k).wait_recv()
            for j in range(1, here.cols):
                copy = self.col_copy(arrived, arrived, k, j)
                copy.start()
                self.passes.append(copy)

    def finish(self):
        here = self.here
        for k in range(here.team):
            for j in range(1, here.cols):
                landed = self.slot(k, lax.rem(here.col - j + here.cols, here.cols))
                self.col_copy(landed, landed, k, j).wait_recv()
        for copy in self.passes + self.sends:
            copy.wait_send()
        self.mine.wait()


class Scatter:
    def __init__(self, partial_sum, team, cols):
        self.operands, self.in_specs, self.out_specs = [partial_sum], [VMEM], [VMEM]
        tall, wide = partial_sum.shape[0] // team, partial_sum.shape[1] // cols
        self.out_shape = [jax.ShapeDtypeStruct((tall, wide), jnp.float32)]
        self.scratch = [
            pltpu.VMEM((cols - 1, team, tall, wide), jnp.bfloat16),
            pltpu.VMEM((team - 1, tall, wide), jnp.bfloat16),
            pltpu.VMEM((team - 1, tall, wide), jnp.bfloat16),
            pltpu.SemaphoreType.DMA((team,)),
            pltpu.SemaphoreType.DMA((team,)),
            pltpu.SemaphoreType.DMA((team, cols)),
            pltpu.SemaphoreType.DMA((team, cols)),
        ]

    def bind(self, here, x_ref, o_ref, inbox, stage, land, send, recv, pass_send, pass_recv):
        self.here, self.x_ref, self.o_ref = here, x_ref, o_ref
        self.inbox, self.stage, self.land = inbox, stage, land
        self.send, self.recv = send, recv
        self.pass_send, self.pass_recv = pass_send, pass_recv

    def part(self, k, side):
        tall, wide = self.o_ref.shape
        origin = lax.rem(self.here.place + k, self.here.team)
        return self.x_ref.at[
            pl.ds(pl.multiple_of(origin * tall, tall), tall),
            pl.ds(pl.multiple_of(side * wide, wide), wide),
        ]

    def start(self):
        here = self.here
        self.order = list(range(1, here.team)) + [0]
        self.passes, self.sends = {}, {}
        for k in self.order:
            for j in range(1, here.cols):
                self.passes[k, j] = remote(
                    self.part(k, here.others[j]),
                    self.inbox.at[j - 1, k],
                    self.pass_send.at[k, j],
                    self.pass_recv.at[k, j],
                    (here.row, here.others[j]),
                )
                self.passes[k, j].start()

    def middle(self):
        here = self.here
        for k in self.order:
            total = self.part(k, here.col)[...].astype(jnp.float32)
            for j in range(1, here.cols):
                self.passes[k, j].wait_recv()
                total = total + self.inbox[j - 1, k].astype(jnp.float32)
            if k:
                self.stage[k - 1] = total.astype(jnp.bfloat16)
                self.sends[k] = remote(
                    self.stage.at[k - 1],
                    self.land.at[k - 1],
                    self.send.at[k],
                    self.recv.at[k],
                    (here.mates[k], here.col),
                )
                self.sends[k].start()
            else:
                self.o_ref[...] = total

    def finish(self):
        for k in self.sends:
            self.sends[k].wait_recv()
            self.o_ref[...] += self.land[k - 1].astype(jnp.float32)
        for copy in list(self.passes.values()) + list(self.sends.values()):
            copy.wait_send()


class Wide:
    def __init__(self, blocks, team, cols, outward):
        rows = team * cols
        self.outward = outward
        self.operands, self.in_specs, self.out_specs = [blocks], [ANY], [ANY]
        self.out_shape = [jax.ShapeDtypeStruct((rows,) + blocks.shape[1:], blocks.dtype)]
        self.scratch = [
            pltpu.SemaphoreType.DMA((rows,)),
            pltpu.SemaphoreType.DMA((rows,)),
            pltpu.SemaphoreType.DMA((1,)),
        ]

    def bind(self, here, x_ref, o_ref, send, recv, own):
        self.here, self.x_ref, self.o_ref = here, x_ref, o_ref
        self.send, self.recv, self.own = send, recv, own

    def source(self, peer):
        return self.x_ref.at[lax.rem(peer, self.here.team) if self.outward else peer]

    def copy(self, source, target, k):
        device = (self.here.peers[k], self.here.col)
        return remote(source, target, self.send.at[k], self.recv.at[k], device)

    def start(self):
        here = self.here
        mine = self.o_ref.at[here.row]
        self.copies = [
            self.copy(self.source(here.peers[k]), mine, k) for k in range(1, here.rows)
        ]
        self.mine = pltpu.make_async_copy(self.source(here.row), mine, self.own.at[0])
        for copy in self.copies + [self.mine]:
            copy.start()

    def middle(self):
        pass

    def finish(self):
        here = self.here
        for k in range(1, here.rows):
            landed = self.o_ref.at[lax.rem(here.row - k + here.rows, here.rows)]
            self.copy(landed, landed, k).wait_recv()
        for copy in self.copies:
            copy.wait_send()
        self.mine.wait()


class Tall:
    def __init__(self, block, team, cols, outward):
        self.outward = outward
        self.operands, self.in_specs, self.out_specs = [block], [ANY], [ANY]
        self.out_shape = [jax.ShapeDtypeStruct((cols,) + block.shape[-2:], block.dtype)]
        self.scratch = [
            pltpu.SemaphoreType.DMA((cols,)),
            pltpu.SemaphoreType.DMA((cols,)),
            pltpu.SemaphoreType.DMA((1,)),
        ]

    def bind(self, here, x_ref, o_ref, send, recv, own):
        self.here, self.x_ref, self.o_ref = here, x_ref, o_ref
        self.send, self.recv, self.own = send, recv, own
        self.home = here.group == here.col

    def target(self, m):
        here = self.here
        if self.outward:
            return lax.rem(here.group + m, here.cols) * here.team + here.place, here.group
        return here.col * here.team + here.place, lax.rem(here.col + m, here.cols)

    def copy(self, m):
        here = self.here
        if self.outward:
            source, index = self.x_ref, here.col
        else:
            source, index = self.x_ref.at[lax.rem(here.col + m, here.cols)], here.group
        return remote(
            source, self.o_ref.at[index], self.send.at[m], self.recv.at[index], self.target(m)
        )

    def mine(self):
        source = self.x_ref if self.outward else self.x_ref.at[self.here.col]
        return pltpu.make_async_copy(source, self.o_ref.at[self.here.col], self.own.at[0])

    def start(self):
        for m in range(1, self.here.cols):
            self.copy(m).start()
        pl.when(self.home)(lambda: self.mine().start())
        pl.when(jnp.logical_not(self.home))(lambda: self.copy(0).start())

    def middle(self):
        pass

    def finish(self):
        here = self.here
        for j in range(here.cols):
            landed = self.o_ref.at[j]
            arriving = remote(landed, landed, self.send.at[0], self.recv.at[j], self.target(1))
            own = jnp.logical_and(self.home, here.col == j)
            pl.when(own)(lambda: self.mine().wait())
            pl.when(jnp.logical_not(own))(lambda arriving=arriving: arriving.wait_recv())
        for m in range(1, here.cols):
            self.copy(m).wait_send()
        pl.when(jnp.logical_not(self.home))(lambda: self.copy(0).wait_send())


class Totals:
    def __init__(self, few, factor, scattered, rows):
        self.scattered = scattered
        self.operands, self.in_specs, self.out_specs = [few, factor], [VMEM, VMEM], [VMEM]
        self.out_shape = [jax.ShapeDtypeStruct(few.shape, few.dtype)]
        self.scratch = [
            pltpu.VMEM(few.shape, few.dtype),
            pltpu.VMEM((rows,) + few.shape, few.dtype),
            pltpu.SemaphoreType.DMA((rows,)),
            pltpu.SemaphoreType.DMA((rows,)),
        ]

    def bind(self, here, few_ref, factor_ref, o_ref, out_box, land, send, recv):
        self.here, self.few_ref, self.factor_ref, self.o_ref = here, few_ref, factor_ref, o_ref
        self.out_box, self.land, self.send, self.recv = out_box, land, send, recv

    def start(self):
        pass

    def middle(self):
        pass

    def copy(self, source, target, k):
        device = (self.here.peers[k], self.here.col)
        return remote(source, target, self.send.at[k], self.recv.at[k], device)

    def finish(self):
        here = self.here
        last = self.few_ref.shape[0] - 1
        made = jnp.sum(self.scattered.o_ref[...] * self.factor_ref[...], axis=0, keepdims=True)
        self.out_box[...] = self.few_ref[...]
        self.out_box[last:] = made
        copies = [
            self.copy(self.out_box, self.land.at[here.row], k) for k in range(1, here.rows)
        ]
        for copy in copies:
            copy.start()
        self.land[here.row] = self.out_box[...]
        for k in range(1, here.rows):
            landed = self.land.at[lax.rem(here.row - k + here.rows, here.rows)]
            self.copy(landed, landed, k).wait_recv()
        total = self.land[0]
        for k in range(1, here.rows):
            total = total + self.land[k]
        self.o_ref[...] = total
        for copy in copies:
            copy.wait_send()


def together_kernel(team, cols, parts, *refs):
    here = Here(team, cols)
    refs = list(refs)

    def take(counts):
        return [[refs.pop(0) for _ in range(count)] for count in counts]

    ins = take([len(part.operands) for part in parts])
    outs = take([len(part.out_shape) for part in parts])
    scratch = take([len(part.scratch) for part in parts])
    for part, a, b, c in zip(parts, ins, outs, scratch):
        part.bind(here, *a, *b, *c)
    here.greet()
    for part in parts:
        part.start()
    for part in parts:
        part.middle()
    for part in parts:
        part.finish()


def together(identity, team, cols, *parts):
    return pl.pallas_call(
        functools.partial(together_kernel, team, cols, parts),
        out_shape=[shape for part in parts for shape in part.out_shape],
        in_specs=[spec for part in parts for spec in part.in_specs],
        out_specs=[spec for part in parts for spec in part.out_specs],
        scratch_shapes=[shape for part in parts for shape in part.scratch],
        compiler_params=pltpu.CompilerParams(
            collective_id=identity, has_side_effects=True, vmem_limit_bytes=32 * 2**20
        ),
    )(*[operand for part in parts for operand in part.operands])


def dot(a, b, a_dim, b_dim, kind=jnp.float32):
    out = lax.dot_general(
        a, b, (((a_dim,), (b_dim,)), ((), ())), preferred_element_type=jnp.float32
    )
    return out.astype(kind)


def cuts(whole):
    first, second = whole // 384 * 128, whole // 192 * 128
    return ((0, first), (first, second), (second, whole))


def teams(
    tokens,
    segments,
    first_gain,
    in_weight,
    conv_kernel,
    out_weight,
    second_gain,
    gate_weight,
    up_weight,
    down_weight,
    cotangent,
):
    bf = jnp.bfloat16
    rows, cols = lax.axis_size("row"), lax.axis_size("col")
    team = rows // cols
    row, col = lax.axis_index("row"), lax.axis_index("col")
    place, group = lax.rem(row, team), lax.div(row, team)
    depth, _, width = in_weight.shape
    inner = gate_weight.shape[1]
    thin, part = width // team, inner // team
    held = tokens.shape[0] * team
    blocks = in_weight.reshape(depth, 3, team, thin).transpose(2, 0, 1, 3)
    wide = jnp.concatenate(
        [
            blocks.reshape(team, depth, 3 * thin),
            gate_weight.reshape(depth, team, part).transpose(1, 0, 2),
            up_weight.reshape(depth, team, part).transpose(1, 0, 2),
        ],
        axis=2,
    )
    pieces = [wide[:, :, start:stop] for start, stop in cuts(wide.shape[2])]
    tok_float = tokens.astype(jnp.float32)
    gain_one = first_gain.astype(jnp.float32)
    gain_two = second_gain.astype(jnp.float32)
    kernel = lax.dynamic_slice_in_dim(conv_kernel, place * thin, thin, 1).astype(jnp.float32)
    inv_one = squares_inverse(tok_float)
    normed_one = (tok_float * inv_one * gain_one).astype(bf)

    normed_full, first_wide, out_blocks = together(
        1,
        team,
        cols,
        Gather(normed_one, team, cols),
        Wide(pieces[0], team, cols, True),
        Tall(out_weight, team, cols, True),
    )
    first_wide = first_wide.reshape(rows * depth, -1)
    in_part = first_wide[:, : 3 * thin]
    out_part = out_blocks.transpose(1, 0, 2).reshape(depth, cols * width)

    projected = dot(normed_full, in_part, 1, 0)
    b_part = projected[:, :thin]
    c_part = projected[:, thin : 2 * thin]
    x_part = projected[:, 2 * thin :]
    gated = b_part * x_part
    padded = jnp.concatenate(
        [jnp.full((2,), -1, jnp.int32), segments, jnp.full((2,), -2, jnp.int32)]
    )
    window = lax.dynamic_slice_in_dim(padded, group * held, held + 4)
    own_ids = window[2 : held + 2]
    same_one = (own_ids == window[1 : held + 1]).astype(jnp.float32)[:, None]
    same_two = (own_ids == window[0:held]).astype(jnp.float32)[:, None]
    after_one = (window[3 : held + 3] == own_ids).astype(jnp.float32)[:, None]
    after_two = (window[4 : held + 4] == own_ids).astype(jnp.float32)[:, None]
    earlier = shifted(gated[held - 2 :], "row", team)
    extended = jnp.concatenate([earlier, gated], axis=0)
    back_one = extended[1 : held + 1] * same_one
    back_two = extended[0:held] * same_two
    mixed = kernel[0] * gated + kernel[1] * back_one + kernel[2] * back_two
    conv_out = (c_part * mixed).astype(bf)
    attended, cot_full, second_wide = together(
        2,
        team,
        cols,
        Scatter(dot(conv_out, out_part, 1, 0, bf), team, cols),
        Gather(cotangent, team, cols),
        Wide(pieces[1], team, cols, True),
    )
    middle = tok_float + attended
    inv_two = squares_inverse(middle)
    normed_two = (middle * inv_two * gain_two).astype(bf)
    two_full, third_wide, down_blocks = together(
        3,
        team,
        cols,
        Gather(normed_two, team, cols),
        Wide(pieces[2], team, cols, True),
        Tall(down_weight, team, cols, True),
    )
    down_part = down_blocks.transpose(1, 0, 2).reshape(part, cols * width)
    pair_part = jnp.concatenate(
        [
            first_wide[:, 3 * thin :],
            second_wide.reshape(rows * depth, -1),
            third_wide.reshape(rows * depth, -1),
        ],
        axis=1,
    )
    both = dot(two_full, pair_part, 1, 0)
    gate_value, up_value = both[:, :part], both[:, part:]
    sigma = jax.nn.sigmoid(gate_value)
    activated = gate_value * sigma
    hidden = (activated * up_value).astype(bf)
    hidden_grad = dot(cot_full, down_part, 1, 1)
    gate_grad = hidden_grad * up_value * sigma * (1.0 + gate_value * (1.0 - sigma))
    up_grad = hidden_grad * activated
    pair_grad = jnp.concatenate([gate_grad.astype(bf), up_grad.astype(bf)], axis=1)
    edges = cuts(3 * thin + 2 * part)
    pair_weight_grad = dot(two_full, pair_grad, 0, 0, bf)
    grad_pieces = [
        pair_weight_grad[:, max(start - 3 * thin, 0) : stop - 3 * thin].reshape(rows, depth, -1)
        for start, stop in edges
    ]
    down_grad = dot(hidden, cot_full, 0, 0, bf)
    normed_two_grad, third_back, down_back = together(
        4,
        team,
        cols,
        Scatter(dot(pair_grad, pair_part, 1, 1, bf), team, cols),
        Wide(grad_pieces[2], team, cols, False),
        Tall(down_grad.reshape(part, cols, width).transpose(1, 0, 2), team, cols, False),
    )
    middle_back, gain_two_local = norm_backward(normed_two_grad, gain_two, middle, inv_two)
    middle_grad = cotangent.astype(jnp.float32) + middle_back
    branch_out, attended_grad, second_back = together(
        5,
        team,
        cols,
        Scatter(dot(hidden, down_part, 1, 0, bf), team, cols),
        Gather(middle_grad.astype(bf), team, cols),
        Wide(grad_pieces[1], team, cols, False),
    )
    block_out = (middle + branch_out).astype(bf)
    conv_grad = dot(attended_grad, out_part, 1, 1)
    c_grad = conv_grad * mixed
    mixed_grad = conv_grad * c_part
    later = shifted(mixed_grad[0:2], "row", -team)
    ahead = jnp.concatenate([mixed_grad, later], axis=0)
    gated_grad = (
        kernel[0] * mixed_grad
        + kernel[1] * after_one * ahead[1 : held + 1]
        + kernel[2] * after_two * ahead[2 : held + 2]
    )
    kernel_local = jnp.stack(
        [
            jnp.sum(mixed_grad * gated, axis=0),
            jnp.sum(mixed_grad * back_one, axis=0),
            jnp.sum(mixed_grad * back_two, axis=0),
        ]
    )
    kernel_local = lax.dynamic_update_slice_in_dim(
        jnp.zeros((3, width), jnp.float32), kernel_local, place * thin, 1
    )
    projected_grad = jnp.concatenate(
        [
            (gated_grad * x_part).astype(bf),
            c_grad.astype(bf),
            (gated_grad * b_part).astype(bf),
        ],
        axis=1,
    )
    in_weight_grad = dot(normed_full, projected_grad, 0, 0, bf).reshape(rows, depth, 3 * thin)
    out_grad = dot(conv_out, attended_grad, 0, 0, bf)
    few = jnp.concatenate(
        [gain_two_local[None], kernel_local, jnp.zeros((4, width), jnp.float32)], axis=0
    )
    scattered = Scatter(dot(projected_grad, in_part, 1, 1, bf), team, cols)
    normed_one_grad, totals, first_back, out_back = together(
        6,
        team,
        cols,
        scattered,
        Totals(few, tok_float * inv_one, scattered, rows),
        Wide(jnp.concatenate([in_weight_grad, grad_pieces[0]], axis=2), team, cols, False),
        Tall(out_grad.reshape(depth, cols, width).transpose(1, 0, 2), team, cols, False),
    )
    token_back, _ = norm_backward(normed_one_grad, gain_one, tok_float, inv_one)
    tokens_grad = middle_grad + token_back
    wide_sum = jnp.concatenate(
        [
            jnp.sum(back.astype(jnp.float32).reshape(cols, team, depth, -1), axis=0)
            for back in (first_back, second_back, third_back)
        ],
        axis=2,
    )
    in_grad = (
        wide_sum[:, :, : 3 * thin]
        .reshape(team, depth, 3, thin)
        .transpose(1, 2, 0, 3)
        .reshape(in_weight.shape)
    )
    gate_out = wide_sum[:, :, 3 * thin : 3 * thin + part].transpose(1, 0, 2).reshape(depth, inner)
    up_out = wide_sum[:, :, 3 * thin + part :].transpose(1, 0, 2).reshape(depth, inner)
    return (
        block_out,
        tokens_grad,
        totals[7],
        in_grad,
        totals[1:4],
        jnp.sum(out_back.astype(jnp.float32), axis=0),
        totals[0],
        gate_out,
        up_out,
        jnp.sum(down_back.astype(jnp.float32), axis=0),
    )


def solution(mesh):
    in_specs = (
        P("row", "col"),
        P(),
        P("col"),
        P("row", None, "col"),
        P(None, "col"),
        P("row", "col"),
        P("col"),
        P("row", "col"),
        P("row", "col"),
        P("row", "col"),
        P("row", "col"),
    )
    out_specs = (
        P("row", "col"),
        P("row", "col"),
        P("col"),
        P("row", None, "col"),
        P(None, "col"),
        P("row", "col"),
        P("col"),
        P("row", "col"),
        P("row", "col"),
        P("row", "col"),
    )
    rows, cols = mesh.shape["row"], mesh.shape["col"]
    shared = cols > 1 and rows % cols == 0 and rows // cols > 1
    body = teams if shared else local
    return jax.shard_map(body, mesh=mesh, in_specs=in_specs, out_specs=out_specs, check_vma=False)
```

```python
import functools

import jax
import jax.numpy as jnp
from jax import lax
from jax.experimental import pallas as pl
from jax.experimental.pallas import tpu as pltpu
from jax.sharding import PartitionSpec as P

D = 1024


epsilon = 1e-05


def shifted(block, axis, distance):
    devices = range(lax.axis_size(axis))
    route = [(i - distance, i) for i in devices if i - distance in devices]
    return lax.ppermute(block, axis, route)


def widen(values):
    return lax.all_gather(values, "col", axis=1, tiled=True)


def squares_inverse(values):
    total = lax.psum(jnp.sum(values * values, axis=1), "col")
    return lax.rsqrt(total / D + epsilon)[:, None]


def norm_backward(grad, gain, values, inverse):
    scaled = grad * gain
    total = lax.psum(jnp.sum(scaled * values, axis=1), "col")
    back = inverse * scaled - values * inverse**3 * (total[:, None] / D)
    return (back, jnp.sum(grad * values * inverse, axis=0))


def project(left, weight):
    return jnp.einsum("td,dkc->tkc", left, weight, preferred_element_type=jnp.float32)


def pull(grad, weight):
    partial_sum = jnp.einsum("tkc,dkc->td", grad, weight, preferred_element_type=jnp.float32)
    return lax.psum_scatter(partial_sum, "col", scatter_dimension=1, tiled=True)


def weight_terms(left, grad):
    return lax.psum_scatter(
        jnp.einsum("tr,tkc->rkc", left, grad, preferred_element_type=jnp.float32),
        "row",
        scatter_dimension=0,
        tiled=True,
    )


def local(
    tokens,
    segments,
    first_gain,
    in_weight,
    conv_kernel,
    out_weight,
    second_gain,
    gate_weight,
    up_weight,
    down_weight,
    cotangent,
):
    rows_here = tokens.shape[0]
    tok_float = tokens.astype(jnp.float32)
    gain_one = first_gain.astype(jnp.float32)
    gain_two = second_gain.astype(jnp.float32)
    kernel = conv_kernel.astype(jnp.float32)
    in_full, out_full, gate_full, up_full, down_full = (
        lax.all_gather(in_weight, "row", axis=0, tiled=True),
        lax.all_gather(out_weight, "row", axis=0, tiled=True),
        lax.all_gather(gate_weight, "row", axis=0, tiled=True),
        lax.all_gather(up_weight, "row", axis=0, tiled=True),
        lax.all_gather(down_weight, "row", axis=0, tiled=True),
    )
    pair_weights = jnp.stack([gate_full, up_full], axis=1)
    inv_one = squares_inverse(tok_float)
    normed_one = (tok_float * inv_one * gain_one).astype(jnp.bfloat16)
    normed_one_full = widen(normed_one)
    projected = project(normed_one_full, in_full)
    b_part = projected[:, 0]
    c_part = projected[:, 1]
    x_part = projected[:, 2]
    gated = b_part * x_part
    first_row = lax.axis_index("row") * rows_here
    padded = jnp.concatenate(
        [jnp.full((2,), -1, jnp.int32), segments, jnp.full((2,), -2, jnp.int32)]
    )
    window = lax.dynamic_slice_in_dim(padded, first_row, rows_here + 4)
    own_ids = window[2 : rows_here + 2]
    same_one = (own_ids == window[1 : rows_here + 1]).astype(jnp.float32)[:, None]
    same_two = (own_ids == window[0:rows_here]).astype(jnp.float32)[:, None]
    after_one = (window[3 : rows_here + 3] == own_ids).astype(jnp.float32)[:, None]
    after_two = (window[4 : rows_here + 4] == own_ids).astype(jnp.float32)[:, None]
    earlier = shifted(gated[rows_here - 2 :], "row", 1)
    extended = jnp.concatenate([earlier, gated], axis=0)
    back_one = extended[1 : rows_here + 1] * same_one
    back_two = extended[0:rows_here] * same_two
    mixed = kernel[0] * gated + kernel[1] * back_one + kernel[2] * back_two
    conv_out = (c_part * mixed).astype(jnp.bfloat16)
    conv_full = widen(conv_out)
    attended = project(conv_full, out_full[:, None, :])[:, 0]
    middle = tok_float + attended
    inv_two = squares_inverse(middle)
    normed_two = (middle * inv_two * gain_two).astype(jnp.bfloat16)
    normed_two_full = widen(normed_two)
    both_values = project(normed_two_full, pair_weights)
    gate_value = both_values[:, 0]
    up_value = both_values[:, 1]
    sigma = jax.nn.sigmoid(gate_value)
    activated = gate_value * sigma
    hidden = (activated * up_value).astype(jnp.bfloat16)
    hidden_full = widen(hidden)
    branch_out = project(hidden_full, down_full[:, None, :])[:, 0]
    block_out = (middle + branch_out).astype(jnp.bfloat16)
    cot_three = cotangent[:, None, :]
    hidden_grad = pull(cot_three, down_full[:, None, :])
    down_grad = weight_terms(hidden_full, cot_three)[:, 0]
    gate_grad = hidden_grad * up_value * sigma * (1.0 + gate_value * (1.0 - sigma))
    up_grad = hidden_grad * activated
    pair_grad = jnp.stack([gate_grad, up_grad], axis=1).astype(jnp.bfloat16)
    normed_two_grad = pull(pair_grad, pair_weights)
    pair_weight_grad = weight_terms(normed_two_full, pair_grad)
    middle_back, gain_two_local = norm_backward(normed_two_grad, gain_two, middle, inv_two)
    middle_grad = cotangent.astype(jnp.float32) + middle_back
    attended_grad = middle_grad.astype(jnp.bfloat16)[:, None, :]
    conv_grad = pull(attended_grad, out_full[:, None, :])
    out_grad = weight_terms(conv_full, attended_grad)[:, 0]
    c_grad = conv_grad * mixed
    mixed_grad = conv_grad * c_part
    later = shifted(mixed_grad[0:2], "row", -1)
    ahead = jnp.concatenate([mixed_grad, later], axis=0)
    gated_grad = (
        kernel[0] * mixed_grad
        + kernel[1] * after_one * ahead[1 : rows_here + 1]
        + kernel[2] * after_two * ahead[2 : rows_here + 2]
    )
    kernel_local = jnp.stack(
        [
            jnp.sum(mixed_grad * gated, axis=0),
            jnp.sum(mixed_grad * back_one, axis=0),
            jnp.sum(mixed_grad * back_two, axis=0),
        ]
    )
    projected_grad = jnp.stack([gated_grad * x_part, c_grad, gated_grad * b_part], axis=1).astype(
        jnp.bfloat16
    )
    normed_one_grad = pull(projected_grad, in_full)
    in_grad = weight_terms(normed_one_full, projected_grad)
    token_back, gain_one_local = norm_backward(normed_one_grad, gain_one, tok_float, inv_one)
    tokens_grad = middle_grad + token_back
    gain_one_grad, kernel_grad, gain_two_grad = lax.psum(
        (gain_one_local, kernel_local, gain_two_local), "row"
    )
    return (
        block_out,
        tokens_grad,
        gain_one_grad,
        in_grad,
        kernel_grad,
        out_grad,
        gain_two_grad,
        pair_weight_grad[:, 0],
        pair_weight_grad[:, 1],
        down_grad,
    )


MESH = pl.DeviceIdType.MESH
VMEM = pl.BlockSpec(memory_space=pltpu.VMEM)
ANY = pl.BlockSpec(memory_space=pl.ANY)


def greet(devices):
    barrier = pltpu.get_barrier_semaphore()
    for device in devices:
        pl.semaphore_signal(barrier, inc=1, device_id=device, device_id_type=MESH)
    pl.semaphore_wait(barrier, len(devices))


def remote(source, target, send, receive, device):
    return pltpu.make_async_remote_copy(
        src_ref=source,
        dst_ref=target,
        send_sem=send,
        recv_sem=receive,
        device_id=device,
        device_id_type=MESH,
    )


ORDERS = ((4, 1, 2), (4, 2, 1))


def arrivals(order):
    one, two, three = order
    return (
        (one, (two, three)),
        (two, (three,)),
        (one + two, (three,)),
        (three, ()),
        (one + three, ()),
        (two + three, ()),
        (one + two + three, ()),
    )


class Here:
    def __init__(self, team, cols):
        self.team, self.cols, self.rows = team, cols, team * cols
        self.row, self.col = lax.axis_index("row"), lax.axis_index("col")
        self.place, self.group = lax.rem(self.row, team), lax.div(self.row, team)
        self.others = [None] + [lax.rem(self.col + j, cols) for j in range(1, cols)]
        self.peers = [None] + [lax.rem(self.row + k, self.rows) for k in range(1, self.rows)]

    def flip(self, mask):
        flipped = self.place
        for bit in (1, 2, 4):
            if mask & bit:
                flipped = flipped + bit - 2 * bit * lax.rem(lax.div(self.place, bit), 2)
        return flipped

    def mate(self, mask):
        return self.group * self.team + self.flip(mask), self.col

    def greet(self):
        devices = [(peer, self.col) for peer in self.peers[1:]]
        for m in range(self.cols):
            there = lax.rem(self.group + m, self.cols) * self.team + self.place
            devices += [(there, other) for other in self.others[1:]]
        barrier = pltpu.get_barrier_semaphore()
        for device in devices:
            pl.semaphore_signal(barrier, inc=1, device_id=device, device_id_type=MESH)
        pl.semaphore_wait(barrier, len(devices))


class Gather:
    def __init__(self, block, team, cols):
        self.operands, self.in_specs, self.out_specs = [block], [ANY], [ANY]
        tall, wide = block.shape
        self.out_shape = [jax.ShapeDtypeStruct((tall * team, wide * cols), block.dtype)]
        self.scratch = [
            pltpu.SemaphoreType.DMA((2, team)),
            pltpu.SemaphoreType.DMA((2, team)),
            pltpu.SemaphoreType.DMA((2, team, cols)),
            pltpu.SemaphoreType.DMA((2, team, cols)),
            pltpu.SemaphoreType.DMA((1,)),
        ]

    def bind(self, here, x_ref, o_ref, send, recv, pass_send, pass_recv, own):
        self.here, self.x_ref, self.o_ref = here, x_ref, o_ref
        self.send, self.recv = send, recv
        self.pass_send, self.pass_recv, self.own = pass_send, pass_recv, own

    def slot(self, half, mask, side):
        tall, wide = self.x_ref.shape
        tall = tall // 2
        begin = self.here.flip(mask) * (2 * tall) + half * tall
        return self.o_ref.at[
            pl.ds(pl.multiple_of(begin, tall), tall),
            pl.ds(pl.multiple_of(side * wide, wide), wide),
        ]

    def row_copy(self, source, target, half, mask, step):
        send, recv = self.send.at[half, mask], self.recv.at[half, mask]
        return remote(source, target, send, recv, self.here.mate(step))

    def col_copy(self, source, target, half, mask, j):
        send, recv = self.pass_send.at[half, mask, j], self.pass_recv.at[half, mask, j]
        return remote(source, target, send, recv, (self.here.row, self.here.others[j]))

    def give(self, source, half, mask, steps):
        here = self.here
        landing = self.slot(half, mask, here.col)
        copies = [self.row_copy(source, landing, half, mask + step, step) for step in steps]
        copies += [self.col_copy(source, landing, half, mask, j) for j in range(1, here.cols)]
        for copy in copies:
            copy.start()
        self.copies += copies

    def start(self):
        tall, wide = self.x_ref.shape
        self.copies, self.mine = [], []
        for half, order in enumerate(ORDERS):
            source = self.x_ref.at[pl.ds(half * (tall // 2), tall // 2)]
            self.give(source, half, 0, order)
        tall, wide = self.x_ref.shape
        own = self.o_ref.at[
            pl.ds(pl.multiple_of(self.here.place * tall, tall), tall),
            pl.ds(pl.multiple_of(self.here.col * wide, wide), wide),
        ]
        self.mine = pltpu.make_async_copy(self.x_ref, own, self.own.at[0])
        self.mine.start()

    def stages(self):
        for turn in zip(*(arrivals(order) for order in ORDERS)):
            for half, (mask, steps) in enumerate(turn):
                arrived = self.slot(half, mask, self.here.col)
                self.row_copy(arrived, arrived, half, mask, mask).wait_recv()
                self.give(arrived, half, mask, steps)
            yield

    def finish(self):
        here = self.here
        for half in range(2):
            for mask in range(here.team):
                for j in range(1, here.cols):
                    side = lax.rem(here.col - j + here.cols, here.cols)
                    landed = self.slot(half, mask, side)
                    self.col_copy(landed, landed, half, mask, j).wait_recv()
        for copy in self.copies:
            copy.wait_send()
        self.mine.wait()


class Scatter:
    def __init__(self, partial_sum, team, cols):
        self.operands, self.in_specs, self.out_specs = [partial_sum], [VMEM], [VMEM]
        tall, wide = partial_sum.shape[0] // team, partial_sum.shape[1] // cols
        self.out_shape = [jax.ShapeDtypeStruct((tall, wide), jnp.float32)]
        self.scratch = [
            pltpu.VMEM((cols - 1, team, tall, wide), jnp.bfloat16),
            pltpu.VMEM((team, tall, wide), jnp.float32),
            pltpu.VMEM((team, tall, wide), jnp.bfloat16),
            pltpu.VMEM((team, tall, wide), jnp.bfloat16),
            pltpu.SemaphoreType.DMA((2, team)),
            pltpu.SemaphoreType.DMA((2, team)),
            pltpu.SemaphoreType.DMA((team, cols)),
            pltpu.SemaphoreType.DMA((team, cols)),
        ]

    def bind(self, here, x_ref, o_ref, inbox, total, stage, land, send, recv, *passing):
        self.here, self.x_ref, self.o_ref = here, x_ref, o_ref
        self.inbox, self.total, self.stage, self.land = inbox, total, stage, land
        self.send, self.recv = send, recv
        self.pass_send, self.pass_recv = passing

    def part(self, mask, side):
        tall, wide = self.o_ref.shape
        return self.x_ref.at[
            pl.ds(pl.multiple_of(self.here.flip(mask) * tall, tall), tall),
            pl.ds(pl.multiple_of(side * wide, wide), wide),
        ]

    def start(self):
        here = self.here
        self.order = (7, 3, 6, 5, 2, 1, 4, 0)
        self.passes, self.sends = {}, {}
        for mask in self.order:
            for j in range(1, here.cols):
                self.passes[mask, j] = remote(
                    self.part(mask, here.others[j]),
                    self.inbox.at[j - 1, mask],
                    self.pass_send.at[mask, j],
                    self.pass_recv.at[mask, j],
                    (here.row, here.others[j]),
                )
                self.passes[mask, j].start()

    def lines(self, half):
        tall = self.o_ref.shape[0] // 2
        return pl.ds(half * tall, tall)

    def give(self, half, mask, step):
        lines = self.lines(half)
        self.stage[mask, lines] = self.total[mask, lines].astype(jnp.bfloat16)
        self.sends[half, mask] = remote(
            self.stage.at[mask, lines],
            self.land.at[mask, lines],
            self.send.at[half, mask],
            self.recv.at[half, mask],
            self.here.mate(step),
        )
        self.sends[half, mask].start()

    def take(self, half, mask, step):
        lines = self.lines(half)
        self.sends[half, mask].wait_recv()
        self.total[mask - step, lines] += self.land[mask, lines].astype(jnp.float32)

    def stages(self):
        here = self.here
        for mask in self.order:
            total = self.part(mask, here.col)[...].astype(jnp.float32)
            for j in range(1, here.cols):
                self.passes[mask, j].wait_recv()
                total = total + self.inbox[j - 1, mask].astype(jnp.float32)
            self.total[mask] = total
            for half, order in enumerate(ORDERS):
                if mask & order[2]:
                    self.give(half, mask, order[2])
        yield
        for half, (one, two, three) in enumerate(ORDERS):
            self.take(half, one + two + three, three)
            self.give(half, one + two, two)
        yield
        for half, (one, two, three) in enumerate(ORDERS):
            self.take(half, two + three, three)
            self.give(half, two, two)
        yield
        for half, (one, two, three) in enumerate(ORDERS):
            self.take(half, one + three, three)
            self.take(half, one + two, two)
            self.give(half, one, one)
        yield
        for half, (one, two, three) in enumerate(ORDERS):
            for step in (three, two, one):
                self.take(half, step, step)
        self.o_ref[...] = self.total[0]

    def finish(self):
        for copy in list(self.passes.values()) + list(self.sends.values()):
            copy.wait_send()


class Wide:
    def __init__(self, blocks, team, cols, outward):
        rows = team * cols
        self.outward = outward
        self.operands, self.in_specs, self.out_specs = [blocks], [ANY], [ANY]
        self.out_shape = [jax.ShapeDtypeStruct((rows,) + blocks.shape[1:], blocks.dtype)]
        self.scratch = [
            pltpu.SemaphoreType.DMA((rows,)),
            pltpu.SemaphoreType.DMA((rows,)),
            pltpu.SemaphoreType.DMA((1,)),
        ]

    def bind(self, here, x_ref, o_ref, send, recv, own):
        self.here, self.x_ref, self.o_ref = here, x_ref, o_ref
        self.send, self.recv, self.own = send, recv, own

    def source(self, peer):
        return self.x_ref.at[lax.rem(peer, self.here.team) if self.outward else peer]

    def copy(self, source, target, k):
        device = (self.here.peers[k], self.here.col)
        return remote(source, target, self.send.at[k], self.recv.at[k], device)

    def start(self):
        here = self.here
        mine = self.o_ref.at[here.row]
        self.copies = [
            self.copy(self.source(here.peers[k]), mine, k) for k in range(1, here.rows)
        ]
        self.mine = pltpu.make_async_copy(self.source(here.row), mine, self.own.at[0])
        for copy in self.copies + [self.mine]:
            copy.start()

    def finish(self):
        here = self.here
        for k in range(1, here.rows):
            landed = self.o_ref.at[lax.rem(here.row - k + here.rows, here.rows)]
            self.copy(landed, landed, k).wait_recv()
        for copy in self.copies:
            copy.wait_send()
        self.mine.wait()


class Tall:
    def __init__(self, block, team, cols, outward):
        self.outward = outward
        self.operands, self.in_specs, self.out_specs = [block], [ANY], [ANY]
        self.out_shape = [jax.ShapeDtypeStruct((cols,) + block.shape[-2:], block.dtype)]
        self.scratch = [
            pltpu.SemaphoreType.DMA((cols,)),
            pltpu.SemaphoreType.DMA((cols,)),
            pltpu.SemaphoreType.DMA((1,)),
        ]

    def bind(self, here, x_ref, o_ref, send, recv, own):
        self.here, self.x_ref, self.o_ref = here, x_ref, o_ref
        self.send, self.recv, self.own = send, recv, own
        self.home = here.group == here.col

    def target(self, m):
        here = self.here
        if self.outward:
            return lax.rem(here.group + m, here.cols) * here.team + here.place, here.group
        return here.col * here.team + here.place, lax.rem(here.col + m, here.cols)

    def copy(self, m):
        here = self.here
        if self.outward:
            source, index = self.x_ref, here.col
        else:
            source, index = self.x_ref.at[lax.rem(here.col + m, here.cols)], here.group
        return remote(
            source, self.o_ref.at[index], self.send.at[m], self.recv.at[index], self.target(m)
        )

    def mine(self):
        source = self.x_ref if self.outward else self.x_ref.at[self.here.col]
        return pltpu.make_async_copy(source, self.o_ref.at[self.here.col], self.own.at[0])

    def start(self):
        for m in range(1, self.here.cols):
            self.copy(m).start()
        pl.when(self.home)(lambda: self.mine().start())
        pl.when(jnp.logical_not(self.home))(lambda: self.copy(0).start())

    def finish(self):
        here = self.here
        for j in range(here.cols):
            landed = self.o_ref.at[j]
            arriving = remote(landed, landed, self.send.at[0], self.recv.at[j], self.target(1))
            own = jnp.logical_and(self.home, here.col == j)
            pl.when(own)(lambda: self.mine().wait())
            pl.when(jnp.logical_not(own))(lambda arriving=arriving: arriving.wait_recv())
        for m in range(1, here.cols):
            self.copy(m).wait_send()
        pl.when(jnp.logical_not(self.home))(lambda: self.copy(0).wait_send())


class Totals:
    def __init__(self, few, factor, scattered, rows):
        self.scattered = scattered
        self.operands, self.in_specs, self.out_specs = [few, factor], [VMEM, VMEM], [VMEM]
        self.out_shape = [jax.ShapeDtypeStruct(few.shape, few.dtype)]
        self.scratch = [
            pltpu.VMEM(few.shape, few.dtype),
            pltpu.VMEM((rows,) + few.shape, few.dtype),
            pltpu.SemaphoreType.DMA((rows,)),
            pltpu.SemaphoreType.DMA((rows,)),
        ]

    def bind(self, here, few_ref, factor_ref, o_ref, out_box, land, send, recv):
        self.here, self.few_ref, self.factor_ref, self.o_ref = here, few_ref, factor_ref, o_ref
        self.out_box, self.land, self.send, self.recv = out_box, land, send, recv

    def start(self):
        pass

    def copy(self, source, target, k):
        device = (self.here.peers[k], self.here.col)
        return remote(source, target, self.send.at[k], self.recv.at[k], device)

    def finish(self):
        here = self.here
        last = self.few_ref.shape[0] - 1
        made = jnp.sum(self.scattered.o_ref[...] * self.factor_ref[...], axis=0, keepdims=True)
        self.out_box[...] = self.few_ref[...]
        self.out_box[last:] = made
        copies = [
            self.copy(self.out_box, self.land.at[here.row], k) for k in range(1, here.rows)
        ]
        for copy in copies:
            copy.start()
        self.land[here.row] = self.out_box[...]
        for k in range(1, here.rows):
            landed = self.land.at[lax.rem(here.row - k + here.rows, here.rows)]
            self.copy(landed, landed, k).wait_recv()
        total = self.land[0]
        for k in range(1, here.rows):
            total = total + self.land[k]
        self.o_ref[...] = total
        for copy in copies:
            copy.wait_send()


def together_kernel(team, cols, parts, *refs):
    here = Here(team, cols)
    refs = list(refs)

    def take(counts):
        return [[refs.pop(0) for _ in range(count)] for count in counts]

    ins = take([len(part.operands) for part in parts])
    outs = take([len(part.out_shape) for part in parts])
    scratch = take([len(part.scratch) for part in parts])
    for part, a, b, c in zip(parts, ins, outs, scratch):
        part.bind(here, *a, *b, *c)
    here.greet()
    for part in parts:
        part.start()
    running = [part.stages() for part in parts if hasattr(part, "stages")]
    while running:
        running = [stages for stages in running if next(stages, running) is None]
    for part in parts:
        part.finish()


def together(identity, team, cols, *parts):
    return pl.pallas_call(
        functools.partial(together_kernel, team, cols, parts),
        out_shape=[shape for part in parts for shape in part.out_shape],
        in_specs=[spec for part in parts for spec in part.in_specs],
        out_specs=[spec for part in parts for spec in part.out_specs],
        scratch_shapes=[shape for part in parts for shape in part.scratch],
        compiler_params=pltpu.CompilerParams(
            collective_id=identity, has_side_effects=True, vmem_limit_bytes=32 * 2**20
        ),
    )(*[operand for part in parts for operand in part.operands])


def dot(a, b, a_dim, b_dim, kind=jnp.float32):
    out = lax.dot_general(
        a, b, (((a_dim,), (b_dim,)), ((), ())), preferred_element_type=jnp.float32
    )
    return out.astype(kind)


def cuts(whole):
    first, second = whole // 384 * 128, whole // 192 * 128
    return ((0, first), (first, second), (second, whole))


def teams(
    tokens,
    segments,
    first_gain,
    in_weight,
    conv_kernel,
    out_weight,
    second_gain,
    gate_weight,
    up_weight,
    down_weight,
    cotangent,
):
    bf = jnp.bfloat16
    rows, cols = lax.axis_size("row"), lax.axis_size("col")
    team = rows // cols
    row, col = lax.axis_index("row"), lax.axis_index("col")
    place, group = lax.rem(row, team), lax.div(row, team)
    depth, _, width = in_weight.shape
    inner = gate_weight.shape[1]
    thin, part = width // team, inner // team
    held = tokens.shape[0] * team
    blocks = in_weight.reshape(depth, 3, team, thin).transpose(2, 0, 1, 3)
    wide = jnp.concatenate(
        [
            blocks.reshape(team, depth, 3 * thin),
            gate_weight.reshape(depth, team, part).transpose(1, 0, 2),
            up_weight.reshape(depth, team, part).transpose(1, 0, 2),
        ],
        axis=2,
    )
    pieces = [wide[:, :, start:stop] for start, stop in cuts(wide.shape[2])]
    tok_float = tokens.astype(jnp.float32)
    gain_one = first_gain.astype(jnp.float32)
    gain_two = second_gain.astype(jnp.float32)
    kernel = lax.dynamic_slice_in_dim(conv_kernel, place * thin, thin, 1).astype(jnp.float32)
    inv_one = squares_inverse(tok_float)
    normed_one = (tok_float * inv_one * gain_one).astype(bf)

    normed_full, first_wide, out_blocks = together(
        1,
        team,
        cols,
        Gather(normed_one, team, cols),
        Wide(pieces[0], team, cols, True),
        Tall(out_weight, team, cols, True),
    )
    first_wide = first_wide.reshape(rows * depth, -1)
    in_part = first_wide[:, : 3 * thin]
    out_part = out_blocks.transpose(1, 0, 2).reshape(depth, cols * width)

    projected = dot(normed_full, in_part, 1, 0)
    b_part = projected[:, :thin]
    c_part = projected[:, thin : 2 * thin]
    x_part = projected[:, 2 * thin :]
    gated = b_part * x_part
    padded = jnp.concatenate(
        [jnp.full((2,), -1, jnp.int32), segments, jnp.full((2,), -2, jnp.int32)]
    )
    window = lax.dynamic_slice_in_dim(padded, group * held, held + 4)
    own_ids = window[2 : held + 2]
    same_one = (own_ids == window[1 : held + 1]).astype(jnp.float32)[:, None]
    same_two = (own_ids == window[0:held]).astype(jnp.float32)[:, None]
    after_one = (window[3 : held + 3] == own_ids).astype(jnp.float32)[:, None]
    after_two = (window[4 : held + 4] == own_ids).astype(jnp.float32)[:, None]
    earlier = shifted(gated[held - 2 :], "row", team)
    extended = jnp.concatenate([earlier, gated], axis=0)
    back_one = extended[1 : held + 1] * same_one
    back_two = extended[0:held] * same_two
    mixed = kernel[0] * gated + kernel[1] * back_one + kernel[2] * back_two
    conv_out = (c_part * mixed).astype(bf)
    upper = part // 32 * 16
    attended, cot_full, second_wide, upper_blocks = together(
        2,
        team,
        cols,
        Scatter(dot(conv_out, out_part, 1, 0, bf), team, cols),
        Gather(cotangent, team, cols),
        Wide(pieces[1], team, cols, True),
        Tall(down_weight[:upper], team, cols, True),
    )
    middle = tok_float + attended
    inv_two = squares_inverse(middle)
    normed_two = (middle * inv_two * gain_two).astype(bf)
    two_full, third_wide, down_blocks = together(
        3,
        team,
        cols,
        Gather(normed_two, team, cols),
        Wide(pieces[2], team, cols, True),
        Tall(down_weight[upper:], team, cols, True),
    )
    down_blocks = jnp.concatenate([upper_blocks, down_blocks], axis=1)
    down_part = down_blocks.transpose(1, 0, 2).reshape(part, cols * width)
    pair_part = jnp.concatenate(
        [
            first_wide[:, 3 * thin :],
            second_wide.reshape(rows * depth, -1),
            third_wide.reshape(rows * depth, -1),
        ],
        axis=1,
    )
    both = dot(two_full, pair_part, 1, 0)
    gate_value, up_value = both[:, :part], both[:, part:]
    sigma = jax.nn.sigmoid(gate_value)
    activated = gate_value * sigma
    hidden = (activated * up_value).astype(bf)
    hidden_grad = dot(cot_full, down_part, 1, 1)
    gate_grad = hidden_grad * up_value * sigma * (1.0 + gate_value * (1.0 - sigma))
    up_grad = hidden_grad * activated
    pair_grad = jnp.concatenate([gate_grad.astype(bf), up_grad.astype(bf)], axis=1)
    edges = cuts(3 * thin + 2 * part)
    pair_weight_grad = dot(two_full, pair_grad, 0, 0, bf)
    grad_pieces = [
        pair_weight_grad[:, max(start - 3 * thin, 0) : stop - 3 * thin].reshape(rows, depth, -1)
        for start, stop in edges
    ]
    down_grad = dot(hidden, cot_full, 0, 0, bf)
    down_grad = down_grad.reshape(part, cols, width).transpose(1, 0, 2)
    normed_two_grad, third_back, upper_back = together(
        4,
        team,
        cols,
        Scatter(dot(pair_grad, pair_part, 1, 1, bf), team, cols),
        Wide(grad_pieces[2], team, cols, False),
        Tall(down_grad[:, :upper], team, cols, False),
    )
    middle_back, gain_two_local = norm_backward(normed_two_grad, gain_two, middle, inv_two)
    middle_grad = cotangent.astype(jnp.float32) + middle_back
    branch_out, attended_grad, second_back, lower_back = together(
        5,
        team,
        cols,
        Scatter(dot(hidden, down_part, 1, 0, bf), team, cols),
        Gather(middle_grad.astype(bf), team, cols),
        Wide(grad_pieces[1], team, cols, False),
        Tall(down_grad[:, upper:], team, cols, False),
    )
    block_out = (middle + branch_out).astype(bf)
    conv_grad = dot(attended_grad, out_part, 1, 1)
    c_grad = conv_grad * mixed
    mixed_grad = conv_grad * c_part
    later = shifted(mixed_grad[0:2], "row", -team)
    ahead = jnp.concatenate([mixed_grad, later], axis=0)
    gated_grad = (
        kernel[0] * mixed_grad
        + kernel[1] * after_one * ahead[1 : held + 1]
        + kernel[2] * after_two * ahead[2 : held + 2]
    )
    kernel_local = jnp.stack(
        [
            jnp.sum(mixed_grad * gated, axis=0),
            jnp.sum(mixed_grad * back_one, axis=0),
            jnp.sum(mixed_grad * back_two, axis=0),
        ]
    )
    kernel_local = lax.dynamic_update_slice_in_dim(
        jnp.zeros((3, width), jnp.float32), kernel_local, place * thin, 1
    )
    projected_grad = jnp.concatenate(
        [
            (gated_grad * x_part).astype(bf),
            c_grad.astype(bf),
            (gated_grad * b_part).astype(bf),
        ],
        axis=1,
    )
    in_weight_grad = dot(normed_full, projected_grad, 0, 0, bf).reshape(rows, depth, 3 * thin)
    out_grad = dot(conv_out, attended_grad, 0, 0, bf)
    few = jnp.concatenate(
        [gain_two_local[None], kernel_local, jnp.zeros((4, width), jnp.float32)], axis=0
    )
    scattered = Scatter(dot(projected_grad, in_part, 1, 1, bf), team, cols)
    normed_one_grad, totals, first_back, out_back = together(
        6,
        team,
        cols,
        scattered,
        Totals(few, tok_float * inv_one, scattered, rows),
        Wide(jnp.concatenate([in_weight_grad, grad_pieces[0]], axis=2), team, cols, False),
        Tall(out_grad.reshape(depth, cols, width).transpose(1, 0, 2), team, cols, False),
    )
    token_back, _ = norm_backward(normed_one_grad, gain_one, tok_float, inv_one)
    tokens_grad = middle_grad + token_back
    wide_sum = jnp.concatenate(
        [
            jnp.sum(back.astype(jnp.float32).reshape(cols, team, depth, -1), axis=0)
            for back in (first_back, second_back, third_back)
        ],
        axis=2,
    )
    in_grad = (
        wide_sum[:, :, : 3 * thin]
        .reshape(team, depth, 3, thin)
        .transpose(1, 2, 0, 3)
        .reshape(in_weight.shape)
    )
    gate_out = wide_sum[:, :, 3 * thin : 3 * thin + part].transpose(1, 0, 2).reshape(depth, inner)
    up_out = wide_sum[:, :, 3 * thin + part :].transpose(1, 0, 2).reshape(depth, inner)
    return (
        block_out,
        tokens_grad,
        totals[7],
        in_grad,
        totals[1:4],
        jnp.sum(out_back.astype(jnp.float32), axis=0),
        totals[0],
        gate_out,
        up_out,
        jnp.concatenate(
            [jnp.sum(b.astype(jnp.float32), axis=0) for b in (upper_back, lower_back)], axis=0
        ),
    )


def solution(mesh):
    in_specs = (
        P("row", "col"),
        P(),
        P("col"),
        P("row", None, "col"),
        P(None, "col"),
        P("row", "col"),
        P("col"),
        P("row", "col"),
        P("row", "col"),
        P("row", "col"),
        P("row", "col"),
    )
    out_specs = (
        P("row", "col"),
        P("row", "col"),
        P("col"),
        P("row", None, "col"),
        P(None, "col"),
        P("row", "col"),
        P("col"),
        P("row", "col"),
        P("row", "col"),
        P("row", "col"),
    )
    rows, cols = mesh.shape["row"], mesh.shape["col"]
    shared = cols > 1 and rows == 8 * cols
    body = teams if shared else local
    return jax.shard_map(body, mesh=mesh, in_specs=in_specs, out_specs=out_specs, check_vma=False)
```

```python
import functools

import jax
import jax.numpy as jnp
from jax import lax
from jax.experimental import pallas as pl
from jax.experimental.pallas import tpu as pltpu
from jax.sharding import PartitionSpec as P

D = 1024


epsilon = 1e-05


def shifted(block, axis, distance):
    devices = range(lax.axis_size(axis))
    route = [(i - distance, i) for i in devices if i - distance in devices]
    return lax.ppermute(block, axis, route)


def widen(values):
    return lax.all_gather(values, "col", axis=1, tiled=True)


def squares_inverse(values):
    total = lax.psum(jnp.sum(values * values, axis=1), "col")
    return lax.rsqrt(total / D + epsilon)[:, None]


def norm_backward(grad, gain, values, inverse):
    scaled = grad * gain
    total = lax.psum(jnp.sum(scaled * values, axis=1), "col")
    back = inverse * scaled - values * inverse**3 * (total[:, None] / D)
    return (back, jnp.sum(grad * values * inverse, axis=0))


def project(left, weight):
    return jnp.einsum("td,dkc->tkc", left, weight, preferred_element_type=jnp.float32)


def pull(grad, weight):
    partial_sum = jnp.einsum("tkc,dkc->td", grad, weight, preferred_element_type=jnp.float32)
    return lax.psum_scatter(partial_sum, "col", scatter_dimension=1, tiled=True)


def weight_terms(left, grad):
    return lax.psum_scatter(
        jnp.einsum("tr,tkc->rkc", left, grad, preferred_element_type=jnp.float32),
        "row",
        scatter_dimension=0,
        tiled=True,
    )


def local(
    tokens,
    segments,
    first_gain,
    in_weight,
    conv_kernel,
    out_weight,
    second_gain,
    gate_weight,
    up_weight,
    down_weight,
    cotangent,
):
    rows_here = tokens.shape[0]
    tok_float = tokens.astype(jnp.float32)
    gain_one = first_gain.astype(jnp.float32)
    gain_two = second_gain.astype(jnp.float32)
    kernel = conv_kernel.astype(jnp.float32)
    in_full, out_full, gate_full, up_full, down_full = (
        lax.all_gather(in_weight, "row", axis=0, tiled=True),
        lax.all_gather(out_weight, "row", axis=0, tiled=True),
        lax.all_gather(gate_weight, "row", axis=0, tiled=True),
        lax.all_gather(up_weight, "row", axis=0, tiled=True),
        lax.all_gather(down_weight, "row", axis=0, tiled=True),
    )
    pair_weights = jnp.stack([gate_full, up_full], axis=1)
    inv_one = squares_inverse(tok_float)
    normed_one = (tok_float * inv_one * gain_one).astype(jnp.bfloat16)
    normed_one_full = widen(normed_one)
    projected = project(normed_one_full, in_full)
    b_part = projected[:, 0]
    c_part = projected[:, 1]
    x_part = projected[:, 2]
    gated = b_part * x_part
    first_row = lax.axis_index("row") * rows_here
    padded = jnp.concatenate(
        [jnp.full((2,), -1, jnp.int32), segments, jnp.full((2,), -2, jnp.int32)]
    )
    window = lax.dynamic_slice_in_dim(padded, first_row, rows_here + 4)
    own_ids = window[2 : rows_here + 2]
    same_one = (own_ids == window[1 : rows_here + 1]).astype(jnp.float32)[:, None]
    same_two = (own_ids == window[0:rows_here]).astype(jnp.float32)[:, None]
    after_one = (window[3 : rows_here + 3] == own_ids).astype(jnp.float32)[:, None]
    after_two = (window[4 : rows_here + 4] == own_ids).astype(jnp.float32)[:, None]
    earlier = shifted(gated[rows_here - 2 :], "row", 1)
    extended = jnp.concatenate([earlier, gated], axis=0)
    back_one = extended[1 : rows_here + 1] * same_one
    back_two = extended[0:rows_here] * same_two
    mixed = kernel[0] * gated + kernel[1] * back_one + kernel[2] * back_two
    conv_out = (c_part * mixed).astype(jnp.bfloat16)
    conv_full = widen(conv_out)
    attended = project(conv_full, out_full[:, None, :])[:, 0]
    middle = tok_float + attended
    inv_two = squares_inverse(middle)
    normed_two = (middle * inv_two * gain_two).astype(jnp.bfloat16)
    normed_two_full = widen(normed_two)
    both_values = project(normed_two_full, pair_weights)
    gate_value = both_values[:, 0]
    up_value = both_values[:, 1]
    sigma = jax.nn.sigmoid(gate_value)
    activated = gate_value * sigma
    hidden = (activated * up_value).astype(jnp.bfloat16)
    hidden_full = widen(hidden)
    branch_out = project(hidden_full, down_full[:, None, :])[:, 0]
    block_out = (middle + branch_out).astype(jnp.bfloat16)
    cot_three = cotangent[:, None, :]
    hidden_grad = pull(cot_three, down_full[:, None, :])
    down_grad = weight_terms(hidden_full, cot_three)[:, 0]
    gate_grad = hidden_grad * up_value * sigma * (1.0 + gate_value * (1.0 - sigma))
    up_grad = hidden_grad * activated
    pair_grad = jnp.stack([gate_grad, up_grad], axis=1).astype(jnp.bfloat16)
    normed_two_grad = pull(pair_grad, pair_weights)
    pair_weight_grad = weight_terms(normed_two_full, pair_grad)
    middle_back, gain_two_local = norm_backward(normed_two_grad, gain_two, middle, inv_two)
    middle_grad = cotangent.astype(jnp.float32) + middle_back
    attended_grad = middle_grad.astype(jnp.bfloat16)[:, None, :]
    conv_grad = pull(attended_grad, out_full[:, None, :])
    out_grad = weight_terms(conv_full, attended_grad)[:, 0]
    c_grad = conv_grad * mixed
    mixed_grad = conv_grad * c_part
    later = shifted(mixed_grad[0:2], "row", -1)
    ahead = jnp.concatenate([mixed_grad, later], axis=0)
    gated_grad = (
        kernel[0] * mixed_grad
        + kernel[1] * after_one * ahead[1 : rows_here + 1]
        + kernel[2] * after_two * ahead[2 : rows_here + 2]
    )
    kernel_local = jnp.stack(
        [
            jnp.sum(mixed_grad * gated, axis=0),
            jnp.sum(mixed_grad * back_one, axis=0),
            jnp.sum(mixed_grad * back_two, axis=0),
        ]
    )
    projected_grad = jnp.stack([gated_grad * x_part, c_grad, gated_grad * b_part], axis=1).astype(
        jnp.bfloat16
    )
    normed_one_grad = pull(projected_grad, in_full)
    in_grad = weight_terms(normed_one_full, projected_grad)
    token_back, gain_one_local = norm_backward(normed_one_grad, gain_one, tok_float, inv_one)
    tokens_grad = middle_grad + token_back
    gain_one_grad, kernel_grad, gain_two_grad = lax.psum(
        (gain_one_local, kernel_local, gain_two_local), "row"
    )
    return (
        block_out,
        tokens_grad,
        gain_one_grad,
        in_grad,
        kernel_grad,
        out_grad,
        gain_two_grad,
        pair_weight_grad[:, 0],
        pair_weight_grad[:, 1],
        down_grad,
    )


MESH = pl.DeviceIdType.MESH
VMEM = pl.BlockSpec(memory_space=pltpu.VMEM)
ANY = pl.BlockSpec(memory_space=pl.ANY)


def greet(devices):
    barrier = pltpu.get_barrier_semaphore()
    for device in devices:
        pl.semaphore_signal(barrier, inc=1, device_id=device, device_id_type=MESH)
    pl.semaphore_wait(barrier, len(devices))


def remote(source, target, send, receive, device):
    return pltpu.make_async_remote_copy(
        src_ref=source,
        dst_ref=target,
        send_sem=send,
        recv_sem=receive,
        device_id=device,
        device_id_type=MESH,
    )


ORDERS = ((4, 1, 2), (4, 2, 1))


def arrivals(order):
    one, two, three = order
    return (
        (one, (two, three)),
        (two, (three,)),
        (one + two, (three,)),
        (three, ()),
        (one + three, ()),
        (two + three, ()),
        (one + two + three, ()),
    )


class Here:
    def __init__(self, team, cols):
        self.team, self.cols, self.rows = team, cols, team * cols
        self.row, self.col = lax.axis_index("row"), lax.axis_index("col")
        self.place, self.group = lax.rem(self.row, team), lax.div(self.row, team)
        self.others = [None] + [lax.rem(self.col + j, cols) for j in range(1, cols)]
        self.peers = [None] + [lax.rem(self.row + k, self.rows) for k in range(1, self.rows)]

    def flip(self, mask):
        flipped = self.place
        for bit in (1, 2, 4):
            if mask & bit:
                flipped = flipped + bit - 2 * bit * lax.rem(lax.div(self.place, bit), 2)
        return flipped

    def mate(self, mask):
        return self.group * self.team + self.flip(mask), self.col

    def greet(self):
        devices = [(peer, self.col) for peer in self.peers[1:]]
        for m in range(self.cols):
            there = lax.rem(self.group + m, self.cols) * self.team + self.place
            devices += [(there, other) for other in self.others[1:]]
        barrier = pltpu.get_barrier_semaphore()
        for device in devices:
            pl.semaphore_signal(barrier, inc=1, device_id=device, device_id_type=MESH)
        pl.semaphore_wait(barrier, len(devices))


class Gather:
    def __init__(self, block, team, cols):
        self.operands, self.in_specs, self.out_specs = [block], [ANY], [ANY]
        tall, wide = block.shape
        self.out_shape = [jax.ShapeDtypeStruct((tall * team, wide * cols), block.dtype)]
        self.scratch = [
            pltpu.SemaphoreType.DMA((2, team)),
            pltpu.SemaphoreType.DMA((2, team)),
            pltpu.SemaphoreType.DMA((2, team, cols)),
            pltpu.SemaphoreType.DMA((2, team, cols)),
            pltpu.SemaphoreType.DMA((1,)),
        ]

    def bind(self, here, x_ref, o_ref, send, recv, pass_send, pass_recv, own):
        self.here, self.x_ref, self.o_ref = here, x_ref, o_ref
        self.send, self.recv = send, recv
        self.pass_send, self.pass_recv, self.own = pass_send, pass_recv, own

    def slot(self, half, mask, side):
        tall, wide = self.x_ref.shape
        tall = tall // 2
        begin = self.here.flip(mask) * (2 * tall) + half * tall
        return self.o_ref.at[
            pl.ds(pl.multiple_of(begin, tall), tall),
            pl.ds(pl.multiple_of(side * wide, wide), wide),
        ]

    def row_copy(self, source, target, half, mask, step):
        send, recv = self.send.at[half, mask], self.recv.at[half, mask]
        return remote(source, target, send, recv, self.here.mate(step))

    def col_copy(self, source, target, half, mask, j):
        send, recv = self.pass_send.at[half, mask, j], self.pass_recv.at[half, mask, j]
        return remote(source, target, send, recv, (self.here.row, self.here.others[j]))

    def give(self, source, half, mask, steps):
        here = self.here
        landing = self.slot(half, mask, here.col)
        copies = [self.row_copy(source, landing, half, mask + step, step) for step in steps]
        copies += [self.col_copy(source, landing, half, mask, j) for j in range(1, here.cols)]
        for copy in copies:
            copy.start()
        self.copies += copies

    def start(self):
        tall, wide = self.x_ref.shape
        self.copies, self.mine = [], []
        for half, order in enumerate(ORDERS):
            source = self.x_ref.at[pl.ds(half * (tall // 2), tall // 2)]
            self.give(source, half, 0, order)
        tall, wide = self.x_ref.shape
        own = self.o_ref.at[
            pl.ds(pl.multiple_of(self.here.place * tall, tall), tall),
            pl.ds(pl.multiple_of(self.here.col * wide, wide), wide),
        ]
        self.mine = pltpu.make_async_copy(self.x_ref, own, self.own.at[0])
        self.mine.start()

    def stages(self):
        for turn in zip(*(arrivals(order) for order in ORDERS)):
            for half, (mask, steps) in enumerate(turn):
                arrived = self.slot(half, mask, self.here.col)
                self.row_copy(arrived, arrived, half, mask, mask).wait_recv()
                self.give(arrived, half, mask, steps)
            yield

    def finish(self):
        here = self.here
        for half in range(2):
            for mask in range(here.team):
                for j in range(1, here.cols):
                    side = lax.rem(here.col - j + here.cols, here.cols)
                    landed = self.slot(half, mask, side)
                    self.col_copy(landed, landed, half, mask, j).wait_recv()
        for copy in self.copies:
            copy.wait_send()
        self.mine.wait()


class Scatter:
    def __init__(self, partial_sum, team, cols):
        self.operands, self.in_specs, self.out_specs = [partial_sum], [VMEM], [VMEM]
        tall, wide = partial_sum.shape[0] // team, partial_sum.shape[1] // cols
        self.out_shape = [jax.ShapeDtypeStruct((tall, wide), jnp.float32)]
        self.scratch = [
            pltpu.VMEM((cols - 1, team, tall, wide), jnp.bfloat16),
            pltpu.VMEM((team, tall, wide), jnp.float32),
            pltpu.VMEM((team, tall, wide), jnp.bfloat16),
            pltpu.VMEM((team, tall, wide), jnp.bfloat16),
            pltpu.SemaphoreType.DMA((2, team)),
            pltpu.SemaphoreType.DMA((2, team)),
            pltpu.SemaphoreType.DMA((team, cols)),
            pltpu.SemaphoreType.DMA((team, cols)),
        ]

    def bind(self, here, x_ref, o_ref, inbox, total, stage, land, send, recv, *passing):
        self.here, self.x_ref, self.o_ref = here, x_ref, o_ref
        self.inbox, self.total, self.stage, self.land = inbox, total, stage, land
        self.send, self.recv = send, recv
        self.pass_send, self.pass_recv = passing

    def part(self, mask, side):
        tall, wide = self.o_ref.shape
        return self.x_ref.at[
            pl.ds(pl.multiple_of(self.here.flip(mask) * tall, tall), tall),
            pl.ds(pl.multiple_of(side * wide, wide), wide),
        ]

    def start(self):
        here = self.here
        self.order = (7, 3, 6, 5, 2, 1, 4, 0)
        self.passes, self.sends = {}, {}
        for mask in self.order:
            for j in range(1, here.cols):
                self.passes[mask, j] = remote(
                    self.part(mask, here.others[j]),
                    self.inbox.at[j - 1, mask],
                    self.pass_send.at[mask, j],
                    self.pass_recv.at[mask, j],
                    (here.row, here.others[j]),
                )
                self.passes[mask, j].start()

    def lines(self, half):
        tall = self.o_ref.shape[0] // 2
        return pl.ds(half * tall, tall)

    def give(self, half, mask, step):
        lines = self.lines(half)
        self.stage[mask, lines] = self.total[mask, lines].astype(jnp.bfloat16)
        self.sends[half, mask] = remote(
            self.stage.at[mask, lines],
            self.land.at[mask, lines],
            self.send.at[half, mask],
            self.recv.at[half, mask],
            self.here.mate(step),
        )
        self.sends[half, mask].start()

    def take(self, half, mask, step):
        lines = self.lines(half)
        self.sends[half, mask].wait_recv()
        self.total[mask - step, lines] += self.land[mask, lines].astype(jnp.float32)

    def stages(self):
        here = self.here
        for mask in self.order:
            total = self.part(mask, here.col)[...].astype(jnp.float32)
            for j in range(1, here.cols):
                self.passes[mask, j].wait_recv()
                total = total + self.inbox[j - 1, mask].astype(jnp.float32)
            self.total[mask] = total
            for half, order in enumerate(ORDERS):
                if mask & order[2]:
                    self.give(half, mask, order[2])
        yield
        for half, (one, two, three) in enumerate(ORDERS):
            self.take(half, one + two + three, three)
            self.give(half, one + two, two)
        yield
        for half, (one, two, three) in enumerate(ORDERS):
            self.take(half, two + three, three)
            self.give(half, two, two)
        yield
        for half, (one, two, three) in enumerate(ORDERS):
            self.take(half, one + three, three)
            self.take(half, one + two, two)
            self.give(half, one, one)
        yield
        for half, (one, two, three) in enumerate(ORDERS):
            for step in (three, two, one):
                self.take(half, step, step)
        self.o_ref[...] = self.total[0]

    def finish(self):
        for copy in list(self.passes.values()) + list(self.sends.values()):
            copy.wait_send()


class Wide:
    def __init__(self, blocks, team, cols, outward):
        rows = team * cols
        self.outward = outward
        self.operands, self.in_specs, self.out_specs = [blocks], [ANY], [ANY]
        self.out_shape = [jax.ShapeDtypeStruct((rows,) + blocks.shape[1:], blocks.dtype)]
        self.scratch = [
            pltpu.SemaphoreType.DMA((rows,)),
            pltpu.SemaphoreType.DMA((rows,)),
            pltpu.SemaphoreType.DMA((1,)),
        ]

    def bind(self, here, x_ref, o_ref, send, recv, own):
        self.here, self.x_ref, self.o_ref = here, x_ref, o_ref
        self.send, self.recv, self.own = send, recv, own

    def source(self, peer):
        return self.x_ref.at[lax.rem(peer, self.here.team) if self.outward else peer]

    def copy(self, source, target, k):
        device = (self.here.peers[k], self.here.col)
        return remote(source, target, self.send.at[k], self.recv.at[k], device)

    def start(self):
        here = self.here
        mine = self.o_ref.at[here.row]
        self.copies = [
            self.copy(self.source(here.peers[k]), mine, k) for k in range(1, here.rows)
        ]
        self.mine = pltpu.make_async_copy(self.source(here.row), mine, self.own.at[0])
        for copy in self.copies + [self.mine]:
            copy.start()

    def finish(self):
        here = self.here
        for k in range(1, here.rows):
            landed = self.o_ref.at[lax.rem(here.row - k + here.rows, here.rows)]
            self.copy(landed, landed, k).wait_recv()
        for copy in self.copies:
            copy.wait_send()
        self.mine.wait()


class Tall:
    def __init__(self, block, team, cols, outward):
        self.outward = outward
        self.operands, self.in_specs, self.out_specs = [block], [ANY], [ANY]
        self.out_shape = [jax.ShapeDtypeStruct((cols,) + block.shape[-2:], block.dtype)]
        self.scratch = [
            pltpu.SemaphoreType.DMA((cols,)),
            pltpu.SemaphoreType.DMA((cols,)),
            pltpu.SemaphoreType.DMA((1,)),
        ]

    def bind(self, here, x_ref, o_ref, send, recv, own):
        self.here, self.x_ref, self.o_ref = here, x_ref, o_ref
        self.send, self.recv, self.own = send, recv, own
        self.home = here.group == here.col

    def target(self, m):
        here = self.here
        if self.outward:
            return lax.rem(here.group + m, here.cols) * here.team + here.place, here.group
        return here.col * here.team + here.place, lax.rem(here.col + m, here.cols)

    def copy(self, m):
        here = self.here
        if self.outward:
            source, index = self.x_ref, here.col
        else:
            source, index = self.x_ref.at[lax.rem(here.col + m, here.cols)], here.group
        return remote(
            source, self.o_ref.at[index], self.send.at[m], self.recv.at[index], self.target(m)
        )

    def mine(self):
        source = self.x_ref if self.outward else self.x_ref.at[self.here.col]
        return pltpu.make_async_copy(source, self.o_ref.at[self.here.col], self.own.at[0])

    def start(self):
        for m in range(1, self.here.cols):
            self.copy(m).start()
        pl.when(self.home)(lambda: self.mine().start())
        pl.when(jnp.logical_not(self.home))(lambda: self.copy(0).start())

    def finish(self):
        here = self.here
        for j in range(here.cols):
            landed = self.o_ref.at[j]
            arriving = remote(landed, landed, self.send.at[0], self.recv.at[j], self.target(1))
            own = jnp.logical_and(self.home, here.col == j)
            pl.when(own)(lambda: self.mine().wait())
            pl.when(jnp.logical_not(own))(lambda arriving=arriving: arriving.wait_recv())
        for m in range(1, here.cols):
            self.copy(m).wait_send()
        pl.when(jnp.logical_not(self.home))(lambda: self.copy(0).wait_send())


class Totals:
    def __init__(self, few, factor, scattered, rows):
        self.scattered = scattered
        self.operands, self.in_specs, self.out_specs = [few, factor], [VMEM, VMEM], [VMEM]
        self.out_shape = [jax.ShapeDtypeStruct(few.shape, few.dtype)]
        self.scratch = [
            pltpu.VMEM(few.shape, few.dtype),
            pltpu.VMEM((rows,) + few.shape, few.dtype),
            pltpu.SemaphoreType.DMA((rows,)),
            pltpu.SemaphoreType.DMA((rows,)),
        ]

    def bind(self, here, few_ref, factor_ref, o_ref, out_box, land, send, recv):
        self.here, self.few_ref, self.factor_ref, self.o_ref = here, few_ref, factor_ref, o_ref
        self.out_box, self.land, self.send, self.recv = out_box, land, send, recv

    def start(self):
        pass

    def copy(self, source, target, k):
        device = (self.here.peers[k], self.here.col)
        return remote(source, target, self.send.at[k], self.recv.at[k], device)

    def finish(self):
        here = self.here
        last = self.few_ref.shape[0] - 1
        made = jnp.sum(self.scattered.o_ref[...] * self.factor_ref[...], axis=0, keepdims=True)
        self.out_box[...] = self.few_ref[...]
        self.out_box[last:] = made
        copies = [
            self.copy(self.out_box, self.land.at[here.row], k) for k in range(1, here.rows)
        ]
        for copy in copies:
            copy.start()
        self.land[here.row] = self.out_box[...]
        for k in range(1, here.rows):
            landed = self.land.at[lax.rem(here.row - k + here.rows, here.rows)]
            self.copy(landed, landed, k).wait_recv()
        total = self.land[0]
        for k in range(1, here.rows):
            total = total + self.land[k]
        self.o_ref[...] = total
        for copy in copies:
            copy.wait_send()


def together_kernel(team, cols, parts, *refs):
    here = Here(team, cols)
    refs = list(refs)

    def take(counts):
        return [[refs.pop(0) for _ in range(count)] for count in counts]

    ins = take([len(part.operands) for part in parts])
    outs = take([len(part.out_shape) for part in parts])
    scratch = take([len(part.scratch) for part in parts])
    for part, a, b, c in zip(parts, ins, outs, scratch):
        part.bind(here, *a, *b, *c)
    here.greet()
    staged = [part for part in parts if hasattr(part, "stages")]
    for part in staged:
        part.start()
    running = [part.stages() for part in staged]
    next(running[0])
    for part in parts:
        if part not in staged:
            part.start()
    while running:
        running = [stages for stages in running if next(stages, running) is None]
    for part in parts:
        part.finish()


def together(identity, team, cols, *parts):
    return pl.pallas_call(
        functools.partial(together_kernel, team, cols, parts),
        out_shape=[shape for part in parts for shape in part.out_shape],
        in_specs=[spec for part in parts for spec in part.in_specs],
        out_specs=[spec for part in parts for spec in part.out_specs],
        scratch_shapes=[shape for part in parts for shape in part.scratch],
        compiler_params=pltpu.CompilerParams(
            collective_id=identity, has_side_effects=True, vmem_limit_bytes=32 * 2**20
        ),
    )(*[operand for part in parts for operand in part.operands])


def dot(a, b, a_dim, b_dim, kind=jnp.float32):
    out = lax.dot_general(
        a, b, (((a_dim,), (b_dim,)), ((), ())), preferred_element_type=jnp.float32
    )
    return out.astype(kind)


def cuts(whole):
    first, second = whole // 384 * 128, whole // 192 * 128
    return ((0, first), (first, second), (second, whole))


def teams(
    tokens,
    segments,
    first_gain,
    in_weight,
    conv_kernel,
    out_weight,
    second_gain,
    gate_weight,
    up_weight,
    down_weight,
    cotangent,
):
    bf = jnp.bfloat16
    rows, cols = lax.axis_size("row"), lax.axis_size("col")
    team = rows // cols
    row, col = lax.axis_index("row"), lax.axis_index("col")
    place, group = lax.rem(row, team), lax.div(row, team)
    depth, _, width = in_weight.shape
    inner = gate_weight.shape[1]
    thin, part = width // team, inner // team
    held = tokens.shape[0] * team
    blocks = in_weight.reshape(depth, 3, team, thin).transpose(2, 0, 1, 3)
    wide = jnp.concatenate(
        [
            blocks.reshape(team, depth, 3 * thin),
            gate_weight.reshape(depth, team, part).transpose(1, 0, 2),
            up_weight.reshape(depth, team, part).transpose(1, 0, 2),
        ],
        axis=2,
    )
    pieces = [wide[:, :, start:stop] for start, stop in cuts(wide.shape[2])]
    tok_float = tokens.astype(jnp.float32)
    gain_one = first_gain.astype(jnp.float32)
    gain_two = second_gain.astype(jnp.float32)
    kernel = lax.dynamic_slice_in_dim(conv_kernel, place * thin, thin, 1).astype(jnp.float32)
    inv_one = squares_inverse(tok_float)
    normed_one = (tok_float * inv_one * gain_one).astype(bf)

    normed_full, first_wide, out_blocks = together(
        1,
        team,
        cols,
        Gather(normed_one, team, cols),
        Wide(pieces[0], team, cols, True),
        Tall(out_weight, team, cols, True),
    )
    first_wide = first_wide.reshape(rows * depth, -1)
    in_part = first_wide[:, : 3 * thin]
    out_part = out_blocks.transpose(1, 0, 2).reshape(depth, cols * width)

    projected = dot(normed_full, in_part, 1, 0)
    b_part = projected[:, :thin]
    c_part = projected[:, thin : 2 * thin]
    x_part = projected[:, 2 * thin :]
    gated = b_part * x_part
    padded = jnp.concatenate(
        [jnp.full((2,), -1, jnp.int32), segments, jnp.full((2,), -2, jnp.int32)]
    )
    window = lax.dynamic_slice_in_dim(padded, group * held, held + 4)
    own_ids = window[2 : held + 2]
    same_one = (own_ids == window[1 : held + 1]).astype(jnp.float32)[:, None]
    same_two = (own_ids == window[0:held]).astype(jnp.float32)[:, None]
    after_one = (window[3 : held + 3] == own_ids).astype(jnp.float32)[:, None]
    after_two = (window[4 : held + 4] == own_ids).astype(jnp.float32)[:, None]
    earlier = shifted(gated[held - 2 :], "row", team)
    extended = jnp.concatenate([earlier, gated], axis=0)
    back_one = extended[1 : held + 1] * same_one
    back_two = extended[0:held] * same_two
    mixed = kernel[0] * gated + kernel[1] * back_one + kernel[2] * back_two
    conv_out = (c_part * mixed).astype(bf)
    upper = part // 32 * 16
    attended, cot_full, second_wide, upper_blocks = together(
        2,
        team,
        cols,
        Scatter(dot(conv_out, out_part, 1, 0, bf), team, cols),
        Gather(cotangent, team, cols),
        Wide(pieces[1], team, cols, True),
        Tall(down_weight[:upper], team, cols, True),
    )
    middle = tok_float + attended
    inv_two = squares_inverse(middle)
    normed_two = (middle * inv_two * gain_two).astype(bf)
    two_full, third_wide, down_blocks = together(
        3,
        team,
        cols,
        Gather(normed_two, team, cols),
        Wide(pieces[2], team, cols, True),
        Tall(down_weight[upper:], team, cols, True),
    )
    down_blocks = jnp.concatenate([upper_blocks, down_blocks], axis=1)
    down_part = down_blocks.transpose(1, 0, 2).reshape(part, cols * width)
    pair_part = jnp.concatenate(
        [
            first_wide[:, 3 * thin :],
            second_wide.reshape(rows * depth, -1),
            third_wide.reshape(rows * depth, -1),
        ],
        axis=1,
    )
    both = dot(two_full, pair_part, 1, 0)
    gate_value, up_value = both[:, :part], both[:, part:]
    sigma = jax.nn.sigmoid(gate_value)
    activated = gate_value * sigma
    hidden = (activated * up_value).astype(bf)
    hidden_grad = dot(cot_full, down_part, 1, 1)
    gate_grad = hidden_grad * up_value * sigma * (1.0 + gate_value * (1.0 - sigma))
    up_grad = hidden_grad * activated
    pair_grad = jnp.concatenate([gate_grad.astype(bf), up_grad.astype(bf)], axis=1)
    edges = cuts(3 * thin + 2 * part)
    pair_weight_grad = dot(two_full, pair_grad, 0, 0, bf)
    grad_pieces = [
        pair_weight_grad[:, max(start - 3 * thin, 0) : stop - 3 * thin].reshape(rows, depth, -1)
        for start, stop in edges
    ]
    down_grad = dot(hidden, cot_full, 0, 0, bf)
    down_grad = down_grad.reshape(part, cols, width).transpose(1, 0, 2)
    normed_two_grad, third_back, upper_back = together(
        4,
        team,
        cols,
        Scatter(dot(pair_grad, pair_part, 1, 1, bf), team, cols),
        Wide(grad_pieces[2], team, cols, False),
        Tall(down_grad[:, :upper], team, cols, False),
    )
    middle_back, gain_two_local = norm_backward(normed_two_grad, gain_two, middle, inv_two)
    middle_grad = cotangent.astype(jnp.float32) + middle_back
    branch_out, attended_grad, second_back, lower_back = together(
        5,
        team,
        cols,
        Scatter(dot(hidden, down_part, 1, 0, bf), team, cols),
        Gather(middle_grad.astype(bf), team, cols),
        Wide(grad_pieces[1], team, cols, False),
        Tall(down_grad[:, upper:], team, cols, False),
    )
    block_out = (middle + branch_out).astype(bf)
    conv_grad = dot(attended_grad, out_part, 1, 1)
    c_grad = conv_grad * mixed
    mixed_grad = conv_grad * c_part
    later = shifted(mixed_grad[0:2], "row", -team)
    ahead = jnp.concatenate([mixed_grad, later], axis=0)
    gated_grad = (
        kernel[0] * mixed_grad
        + kernel[1] * after_one * ahead[1 : held + 1]
        + kernel[2] * after_two * ahead[2 : held + 2]
    )
    kernel_local = jnp.stack(
        [
            jnp.sum(mixed_grad * gated, axis=0),
            jnp.sum(mixed_grad * back_one, axis=0),
            jnp.sum(mixed_grad * back_two, axis=0),
        ]
    )
    kernel_local = lax.dynamic_update_slice_in_dim(
        jnp.zeros((3, width), jnp.float32), kernel_local, place * thin, 1
    )
    projected_grad = jnp.concatenate(
        [
            (gated_grad * x_part).astype(bf),
            c_grad.astype(bf),
            (gated_grad * b_part).astype(bf),
        ],
        axis=1,
    )
    in_weight_grad = dot(normed_full, projected_grad, 0, 0, bf).reshape(rows, depth, 3 * thin)
    out_grad = dot(conv_out, attended_grad, 0, 0, bf)
    few = jnp.concatenate(
        [gain_two_local[None], kernel_local, jnp.zeros((4, width), jnp.float32)], axis=0
    )
    scattered = Scatter(dot(projected_grad, in_part, 1, 1, bf), team, cols)
    normed_one_grad, totals, first_back, out_back = together(
        6,
        team,
        cols,
        scattered,
        Totals(few, tok_float * inv_one, scattered, rows),
        Wide(jnp.concatenate([in_weight_grad, grad_pieces[0]], axis=2), team, cols, False),
        Tall(out_grad.reshape(depth, cols, width).transpose(1, 0, 2), team, cols, False),
    )
    token_back, _ = norm_backward(normed_one_grad, gain_one, tok_float, inv_one)
    tokens_grad = middle_grad + token_back
    wide_sum = jnp.concatenate(
        [
            jnp.sum(back.astype(jnp.float32).reshape(cols, team, depth, -1), axis=0)
            for back in (first_back, second_back, third_back)
        ],
        axis=2,
    )
    in_grad = (
        wide_sum[:, :, : 3 * thin]
        .reshape(team, depth, 3, thin)
        .transpose(1, 2, 0, 3)
        .reshape(in_weight.shape)
    )
    gate_out = wide_sum[:, :, 3 * thin : 3 * thin + part].transpose(1, 0, 2).reshape(depth, inner)
    up_out = wide_sum[:, :, 3 * thin + part :].transpose(1, 0, 2).reshape(depth, inner)
    return (
        block_out,
        tokens_grad,
        totals[7],
        in_grad,
        totals[1:4],
        jnp.sum(out_back.astype(jnp.float32), axis=0),
        totals[0],
        gate_out,
        up_out,
        jnp.concatenate(
            [jnp.sum(b.astype(jnp.float32), axis=0) for b in (upper_back, lower_back)], axis=0
        ),
    )


def solution(mesh):
    in_specs = (
        P("row", "col"),
        P(),
        P("col"),
        P("row", None, "col"),
        P(None, "col"),
        P("row", "col"),
        P("col"),
        P("row", "col"),
        P("row", "col"),
        P("row", "col"),
        P("row", "col"),
    )
    out_specs = (
        P("row", "col"),
        P("row", "col"),
        P("col"),
        P("row", None, "col"),
        P(None, "col"),
        P("row", "col"),
        P("col"),
        P("row", "col"),
        P("row", "col"),
        P("row", "col"),
    )
    rows, cols = mesh.shape["row"], mesh.shape["col"]
    shared = cols > 1 and rows == 8 * cols
    body = teams if shared else local
    return jax.shard_map(body, mesh=mesh, in_specs=in_specs, out_specs=out_specs, check_vma=False)
```
